512 devices in a mesh: fsdp: 32 (over y, x, core), expert: 16 (over z).
Axes of the slice: x: 4, y: 4, z: 16, core: 2. Of those that a mesh axis runs over, the one named last changes fastest.
Arguments:
- grad: bfloat16 [16, 7168, 384], P('expert', 'fsdp')
- momentum: float32 [16, 7168, 384], P('expert', 'fsdp'), may hold values from -6 to 6
Outputs:
- new_momentum: float32 [16, 7168, 384], P('expert', 'fsdp')
- update: bfloat16 [16, 7168, 384], P('expert', 'fsdp')
The draws below stay inside these ranges and needn't reach their ends.
All inputs are finite; a program needn't handle non-finite values.
Results may differ from the reference program's by a relative error of at most 0.012.
Values may be sent and summed in bfloat16 or wider, within the bound.
No kernel may reach another device: no remote copies, remote signals or barrier semaphores. Data moves between devices by JAX's collectives and lax.ppermute only.
A program may use at most 64 MiB of HBM per device.

```python
import math
import jax
import jax.numpy as jnp
from jax import lax

D = 7168
R = 384
ITERS = 3
LAYERS = 16


def draw_grad(key, part):
    key = jax.random.fold_in(key, 5)
    first, second, third, fourth = jax.random.split(key, 4)
    block_count = 32
    layer_rank = jax.random.permutation(third, LAYERS).astype(jnp.float32)
    layer_pos = layer_rank / max(LAYERS - 1, 1)
    block_rank = jax.random.permutation(fourth, block_count).astype(jnp.float32)
    column_block = jnp.arange(D, dtype=jnp.int32) // (D // block_count)
    column_pos = jnp.take(block_rank, column_block) / (block_count - 1)
    layer_scale = 3.0 ** layer_pos
    column_scale = 3.0 ** column_pos
    row_scale = jnp.exp(jax.random.uniform(second, (LAYERS, 1, R), jnp.float32, 0.0, math.log(10.0)))
    base = jax.random.normal(first, (LAYERS, D, R), jnp.float32)
    values = base * layer_scale[:, None, None] * column_scale[None, :, None] * row_scale
    return values.astype(jnp.bfloat16)


def level_of(key, shape, pieces, smallest, largest):
    loudness = 1.0
    for axis_at, blocks in pieces:
        steps = jax.random.uniform(jax.random.fold_in(jax.random.fold_in(key, 6), axis_at), (blocks,), jnp.float32, smallest / len(pieces), largest / len(pieces))
        loudness = loudness * jnp.repeat(jnp.exp(steps), shape[axis_at] // blocks).reshape((-1,) + (1,) * (len(shape) - 1 - axis_at))
    return loudness


def gaussian(own_key, shape, spread, bound, cuts=(), held_as=jnp.bfloat16):
    drawn = jax.random.normal(own_key, shape, jnp.float32) * spread
    if len(cuts) > 0:
        drawn = level_of(own_key, shape, cuts, -0.22, 0.18) * drawn
    return jnp.clip(drawn, min=-bound, max=bound).astype(held_as)


def setup_inputs(seed: int = 0) -> dict:
    keys = jax.random.split(jax.random.key(seed), 3)
    return {
        "grad": draw_grad(jax.random.fold_in(keys[2], 71), 0),
        "momentum": gaussian(keys[1], (LAYERS, D, R), 1.0, 6.0, ((0, 16), (1, 32)), jnp.float32),
    }


BETA = 0.95
COEF_A = 3.4445
COEF_B = -4.775
COEF_C = 2.0315

def orthogonal_factor(gram_matrix):
    order = gram_matrix.shape[0]
    identity = jnp.eye(order, dtype=jnp.float32)
    norm_inv = 1.0 / (jnp.sqrt(jnp.trace(gram_matrix)) + 1e-07)
    moment = gram_matrix * (norm_inv * norm_inv)
    factor = identity * norm_inv
    for iteration in range(ITERS):
        square = jnp.dot(moment, moment, precision=lax.Precision.HIGHEST)
        poly = COEF_A * identity + COEF_B * moment + COEF_C * square
        factor = jnp.dot(poly, factor, precision=lax.Precision.HIGHEST)
        moment = jnp.dot(jnp.dot(poly, moment, precision=lax.Precision.HIGHEST), poly, precision=lax.Precision.HIGHEST)
    return factor.astype(jnp.bfloat16)

def reference(grad, momentum):
    grad_full = grad.astype(jnp.float32)
    mean_square = jnp.sum(grad_full * grad_full) / (LAYERS * R * D)
    clip_factor = 1.0 / jnp.sqrt(mean_square + 1e-06)
    new_momentum = BETA * momentum + clip_factor * grad_full
    direction = (clip_factor * grad_full + BETA * new_momentum).astype(jnp.bfloat16)
    step_scale = 0.2 * math.sqrt(max(R, D))

    def one_layer(matrix):
        gram_matrix = jnp.einsum('cn,cm->nm', matrix, matrix, preferred_element_type=jnp.float32)
        factor = orthogonal_factor(gram_matrix)
        product = jnp.dot(matrix, factor.T, preferred_element_type=jnp.float32)
        return (step_scale * product).astype(jnp.bfloat16)
    update = lax.map(one_layer, direction)
    return (new_momentum, update)
```

```python
import math

import jax
import jax.numpy as jnp
from jax import lax
from jax.sharding import PartitionSpec as P

ITERS = 3

BETA = 0.95
COEF_A = 3.4445
COEF_B = -4.775
COEF_C = 2.0315


def orthogonal_factor(gram_matrix):
    order = gram_matrix.shape[0]
    identity = jnp.eye(order, dtype=jnp.float32)
    norm_inv = 1.0 / (jnp.sqrt(jnp.trace(gram_matrix)) + 1e-07)
    moment = gram_matrix * (norm_inv * norm_inv)
    factor = None
    for iteration in range(ITERS):
        square = jnp.dot(moment, moment, precision=lax.Precision.HIGHEST)
        poly = COEF_A * identity + COEF_B * moment + COEF_C * square
        if factor is None:
            factor = poly * norm_inv
        else:
            factor = jnp.dot(poly, factor, precision=lax.Precision.HIGHEST)
        if iteration + 1 < ITERS:
            moment = jnp.dot(
                jnp.dot(poly, moment, precision=lax.Precision.HIGHEST),
                poly,
                precision=lax.Precision.HIGHEST,
            )
    return factor.astype(jnp.bfloat16)


def exchange(blocks, axis):
    return lax.all_to_all(blocks, axis, split_axis=0, concat_axis=0, tiled=True)


def scalar_sum(value, axis):
    size = lax.axis_size(axis)
    rows = exchange(jnp.full((size, 128), value, jnp.float32), axis)
    return jnp.sum(rows[:, 0])


def per_device(grad, momentum):
    grad_full = grad[0].astype(jnp.float32)
    fsdp_count = lax.axis_size("fsdp")
    group_count = lax.axis_size("expert")
    total = scalar_sum(jnp.sum(grad_full * grad_full), "expert")
    total = scalar_sum(total, "fsdp")
    mean_square = total / (grad.size * fsdp_count * group_count)
    clip_factor = 1.0 / jnp.sqrt(mean_square + 1e-06)
    new_momentum = BETA * momentum[0] + clip_factor * grad_full
    direction = (clip_factor * grad_full + BETA * new_momentum).astype(jnp.bfloat16)
    width, row_count = direction.shape
    step_scale = 0.2 * math.sqrt(max(row_count, width * fsdp_count))
    part = jnp.einsum("cn,cm->nm", direction, direction, preferred_element_type=jnp.float32)
    share = row_count // fsdp_count
    mine = jnp.sum(exchange(part.reshape(fsdp_count, share, row_count), "fsdp"), axis=0)
    spread = jnp.broadcast_to(mine[None], (fsdp_count, share, row_count))
    gram_matrix = exchange(spread, "fsdp").reshape(row_count, row_count)
    factor = orthogonal_factor(gram_matrix)
    product = jnp.dot(direction, factor.T, preferred_element_type=jnp.float32)
    update = (step_scale * product).astype(jnp.bfloat16)
    return (new_momentum[None], update[None])


def solution(mesh):
    placed = P("expert", "fsdp", None)
    return jax.shard_map(
        per_device,
        mesh=mesh,
        in_specs=(placed, placed),
        out_specs=(placed, placed),
        check_vma=False,
    )
```

```python
import functools
import math

import jax
import jax.numpy as jnp
from jax import lax
from jax.experimental import pallas as pl
from jax.experimental.pallas import tpu as pltpu
from jax.sharding import PartitionSpec as P

ITERS = 3

BETA = 0.95
COEF_A = 3.4445
COEF_B = -4.775
COEF_C = 2.0315

LANE = 128
SUB = 8
CORES = 2


def dot(a, b):
    return jnp.dot(a, b, preferred_element_type=jnp.float32)


def split(x):
    high = x.astype(jnp.bfloat16)
    return high, (x - high.astype(jnp.float32)).astype(jnp.bfloat16)


def blocks_of(order):
    side = order // LANE
    return [(i, j) for i in range(side) for j in range(i, side)]


def gram_kernel(grad_ref, momentum_ref, keep_ref, send_ref, square_ref):
    core = lax.rem(lax.axis_index("fsdp"), CORES)
    grad = grad_ref[0]
    full = grad.astype(jnp.float32)
    squares = jnp.sum(full * full, axis=0, keepdims=True)
    square_ref[...] = jnp.broadcast_to(jnp.sum(squares, axis=1, keepdims=True), square_ref.shape)
    high, low = split(momentum_ref[0])
    grad_t, high_t, low_t = grad.T, high.T, low.T
    grams = (
        dot(grad_t, grad),
        (dot(grad_t, high) + dot(high_t, grad)) + (dot(grad_t, low) + dot(low_t, grad)),
        dot(high_t, high) + (dot(high_t, low) + dot(low_t, high)),
    )
    chips, rows, _ = keep_ref.shape
    per_gram = rows // len(grams)
    pieces = per_gram // SUB
    blocks = blocks_of(grad.shape[1])
    for which, gram in enumerate(grams):

        def piece(q):
            i, j = blocks[q // (LANE // SUB)]
            top = i * LANE + q % (LANE // SUB) * SUB
            return gram[top : top + SUB, j * LANE : (j + 1) * LANE]

        for chip in range(chips):
            for p in range(pieces):
                first = piece((chip * CORES) * pieces + p)
                second = piece((chip * CORES + 1) * pieces + p)
                at = pl.ds(which * per_gram + p * SUB, SUB)
                keep_ref[chip, at, :] = jnp.where(core == 0, first, second)
                send_ref[chip, at, :] = jnp.where(core == 0, second, first)


def middle_kernel(parts_ref, squares_ref, spread_ref):
    chips, rows, _ = parts_ref.shape
    total = jnp.sum(parts_ref[...], axis=0)
    squares = jnp.sum(squares_ref[...], axis=0, keepdims=True)
    for chip in range(chips):
        spread_ref[chip, :rows, :] = total
        spread_ref[chip, rows:, :] = jnp.broadcast_to(squares, (SUB, LANE))


def product(a, b):
    return dot(a[0], b[0]) + (dot(a[0], b[1]) + dot(a[1], b[0]))


def final_kernel(step_scale, count, mine_ref, other_ref, grad_ref, momentum_ref, new_ref, update_ref, gram_ref):
    core = lax.rem(lax.axis_index("fsdp"), CORES)
    order = grad_ref.shape[2]
    chips, rows, _ = mine_ref.shape
    per_gram = (rows - SUB) // 3
    pieces = per_gram // SUB
    squares = jnp.sum(mine_ref[:, rows - SUB :, :], axis=0) + jnp.sum(other_ref[:, rows - SUB :, :], axis=0)
    clip = 1.0 / jnp.sqrt(squares / count + 1e-06)
    alpha = (1.0 + BETA) * clip
    some = alpha > 0.0
    gain_gg, gain_gm, gain_mm = alpha * alpha, alpha * (BETA * BETA), BETA**4
    blocks = blocks_of(order)
    trace = jnp.zeros((SUB, LANE), jnp.float32)
    for chip in range(chips):
        for p in range(pieces):
            at = [pl.ds(which * per_gram + p * SUB, SUB) for which in range(3)]
            held = [mine_ref[chip, a, :] for a in at]
            came = [other_ref[chip, a, :] for a in at]

            def joined(gg, gm, mm):
                return jnp.where(some, gain_gg * gg + gain_gm * gm, 0.0) + gain_mm * mm

            held, came = joined(*held), joined(*came)
            for c, piece in ((0, jnp.where(core == 0, held, came)), (1, jnp.where(core == 0, came, held))):
                q = (chip * CORES + c) * pieces + p
                i, j = blocks[q // (LANE // SUB)]
                down = q % (LANE // SUB) * SUB
                gram_ref[i * LANE + down : i * LANE + down + SUB, j * LANE : (j + 1) * LANE] = piece
                if i == j:
                    row = lax.broadcasted_iota(jnp.int32, (SUB, LANE), 0) + down
                    col = lax.broadcasted_iota(jnp.int32, (SUB, LANE), 1)
                    trace = trace + jnp.where(row == col, piece, 0.0)
    for i, j in blocks:
        if i < j:
            gram_ref[j * LANE : (j + 1) * LANE, i * LANE : (i + 1) * LANE] = gram_ref[
                i * LANE : (i + 1) * LANE, j * LANE : (j + 1) * LANE
            ].T

    clip = clip[:1, :1]
    grad_full = grad_ref[0].astype(jnp.float32)
    new_momentum = BETA * momentum_ref[0] + clip * grad_full
    new_ref[0] = new_momentum
    direction = (clip * grad_full + BETA * new_momentum).astype(jnp.bfloat16)

    trace = jnp.sum(jnp.sum(trace, axis=0, keepdims=True), axis=1, keepdims=True)
    norm_inv = 1.0 / (jnp.sqrt(trace) + 1e-07)
    moment = gram_ref[...] * (norm_inv * norm_inv)
    row = lax.broadcasted_iota(jnp.int32, (order, order), 0)
    col = lax.broadcasted_iota(jnp.int32, (order, order), 1)
    diagonal = jnp.where(row == col, COEF_A, 0.0)
    factor = None
    for iteration in range(ITERS):
        moment_parts = split(moment)
        poly = diagonal + COEF_B * moment + COEF_C * product(moment_parts, moment_parts)
        poly_parts = split(poly)
        if factor is None:
            factor = poly * norm_inv
        else:
            factor = product(poly_parts, split(factor))
        if iteration + 1 < ITERS:
            moment = product(split(product(poly_parts, moment_parts)), poly_parts)
    update = dot(direction, factor.astype(jnp.bfloat16).T)
    update_ref[0] = (step_scale * update).astype(jnp.bfloat16)


def call(kernel, shapes, scratch=()):
    return pl.pallas_call(
        kernel,
        out_shape=shapes,
        scratch_shapes=scratch,
        compiler_params=pltpu.CompilerParams(vmem_limit_bytes=24 * 2**20),
    )


def per_device(grad, momentum):
    fsdp_count = lax.axis_size("fsdp")
    group_count = lax.axis_size("expert")
    _, width, order = grad.shape
    step_scale = 0.2 * math.sqrt(max(order, width * fsdp_count))
    count = grad.size * fsdp_count * group_count
    chips = fsdp_count // CORES
    share = len(blocks_of(order)) * LANE // fsdp_count
    f32 = jnp.float32
    half = jax.ShapeDtypeStruct((chips, 3 * share, LANE), f32)
    keep, send, square = call(
        gram_kernel, (half, half, jax.ShapeDtypeStruct((group_count, LANE), f32))
    )(grad, momentum)
    squares = lax.all_to_all(square, "expert", split_axis=0, concat_axis=0, tiled=True)
    pairs = [(i, i ^ 1) for i in range(fsdp_count)]
    groups = [[CORES * i + c for i in range(chips)] for c in range(CORES)]
    both = keep + lax.ppermute(send, "fsdp", pairs)

    def exchange(x):
        return lax.all_to_all(x, "fsdp", split_axis=0, concat_axis=0, tiled=True, axis_index_groups=groups)

    spread = call(
        middle_kernel, jax.ShapeDtypeStruct((chips, 3 * share + SUB, LANE), f32)
    )(exchange(both), squares)
    mine = exchange(spread)
    other = lax.ppermute(mine, "fsdp", pairs)
    return call(
        functools.partial(final_kernel, step_scale, count),
        (
            jax.ShapeDtypeStruct(grad.shape, f32),
            jax.ShapeDtypeStruct(grad.shape, jnp.bfloat16),
        ),
        (pltpu.VMEM((order, order), f32),),
    )(mine, other, grad, momentum)


def solution(mesh):
    placed = P("expert", "fsdp", None)
    return jax.shard_map(
        per_device,
        mesh=mesh,
        in_specs=(placed, placed),
        out_specs=(placed, placed),
        check_vma=False,
    )
```

```python
import functools
import math

import jax
import jax.numpy as jnp
from jax import lax
from jax.experimental import pallas as pl
from jax.experimental.pallas import tpu as pltpu
from jax.sharding import PartitionSpec as P

ITERS = 3

BETA = 0.95
COEF_A = 3.4445
COEF_B = -4.775
COEF_C = 2.0315

LANE = 128
SUB = 8
CORES = 2


def dot(a, b):
    return jnp.dot(a, b, preferred_element_type=jnp.float32)


def split(x):
    high = x.astype(jnp.bfloat16)
    return high, (x - high.astype(jnp.float32)).astype(jnp.bfloat16)


def blocks_of(order):
    side = order // LANE
    return [(i, j) for i in range(side) for j in range(i, side)]


def gram_kernel(grad_ref, momentum_ref, parts_ref, square_ref):
    grad = grad_ref[0]
    full = grad.astype(jnp.float32)
    squares = jnp.sum(full * full, axis=0, keepdims=True)
    square_ref[...] = jnp.broadcast_to(jnp.sum(squares, axis=1, keepdims=True), square_ref.shape)
    high, low = split(momentum_ref[0])
    grad_t, high_t, low_t = grad.T, high.T, low.T
    grams = (
        dot(grad_t, grad),
        (dot(grad_t, high) + dot(high_t, grad)) + (dot(grad_t, low) + dot(low_t, grad)),
        dot(high_t, high) + (dot(high_t, low) + dot(low_t, high)),
    )
    devices, rows, _ = parts_ref.shape
    per_gram = rows // len(grams)
    pieces = per_gram // SUB
    blocks = blocks_of(grad.shape[1])
    for which, gram in enumerate(grams):
        for device in range(devices):
            for p in range(pieces):
                q = device * pieces + p
                i, j = blocks[q // (LANE // SUB)]
                top = i * LANE + q % (LANE // SUB) * SUB
                at = pl.ds(which * per_gram + p * SUB, SUB)
                parts_ref[device, at, :] = gram[top : top + SUB, j * LANE : (j + 1) * LANE]


def middle_kernel(parts_ref, squares_ref, spread_ref):
    _, rows, _ = parts_ref.shape
    chips = spread_ref.shape[0]
    total = jnp.sum(parts_ref[...], axis=0)
    squares = jnp.sum(squares_ref[...], axis=0, keepdims=True)
    for chip in range(chips):
        spread_ref[chip, :rows, :] = total
        spread_ref[chip, rows:, :] = jnp.broadcast_to(squares, (SUB, LANE))


def product(a, b):
    return dot(a[0], b[0]) + (dot(a[0], b[1]) + dot(a[1], b[0]))


def final_kernel(step_scale, count, mine_ref, other_ref, grad_ref, momentum_ref, new_ref, update_ref, gram_ref):
    core = lax.rem(lax.axis_index("fsdp"), CORES)
    order = grad_ref.shape[2]
    chips, rows, _ = mine_ref.shape
    per_gram = (rows - SUB) // 3
    pieces = per_gram // SUB
    squares = jnp.sum(mine_ref[:, rows - SUB :, :], axis=0) + jnp.sum(other_ref[:, rows - SUB :, :], axis=0)
    clip = 1.0 / jnp.sqrt(squares / count + 1e-06)
    alpha = (1.0 + BETA) * clip
    some = alpha > 0.0
    gain_gg, gain_gm, gain_mm = alpha * alpha, alpha * (BETA * BETA), BETA**4
    blocks = blocks_of(order)
    trace = jnp.zeros((SUB, LANE), jnp.float32)
    for chip in range(chips):
        for p in range(pieces):
            at = [pl.ds(which * per_gram + p * SUB, SUB) for which in range(3)]
            held = [mine_ref[chip, a, :] for a in at]
            came = [other_ref[chip, a, :] for a in at]

            def joined(gg, gm, mm):
                return jnp.where(some, gain_gg * gg + gain_gm * gm, 0.0) + gain_mm * mm

            held, came = joined(*held), joined(*came)
            for c, piece in ((0, jnp.where(core == 0, held, came)), (1, jnp.where(core == 0, came, held))):
                q = (chip * CORES + c) * pieces + p
                i, j = blocks[q // (LANE // SUB)]
                down = q % (LANE // SUB) * SUB
                gram_ref[i * LANE + down : i * LANE + down + SUB, j * LANE : (j + 1) * LANE] = piece
                if i == j:
                    row = lax.broadcasted_iota(jnp.int32, (SUB, LANE), 0) + down
                    col = lax.broadcasted_iota(jnp.int32, (SUB, LANE), 1)
                    trace = trace + jnp.where(row == col, piece, 0.0)
    for i, j in blocks:
        if i < j:
            gram_ref[j * LANE : (j + 1) * LANE, i * LANE : (i + 1) * LANE] = gram_ref[
                i * LANE : (i + 1) * LANE, j * LANE : (j + 1) * LANE
            ].T

    clip = clip[:1, :1]
    grad_full = grad_ref[0].astype(jnp.float32)
    new_momentum = BETA * momentum_ref[0] + clip * grad_full
    new_ref[0] = new_momentum
    direction = (clip * grad_full + BETA * new_momentum).astype(jnp.bfloat16)

    trace = jnp.sum(jnp.sum(trace, axis=0, keepdims=True), axis=1, keepdims=True)
    norm_inv = 1.0 / (jnp.sqrt(trace) + 1e-07)
    moment = gram_ref[...] * (norm_inv * norm_inv)
    row = lax.broadcasted_iota(jnp.int32, (order, order), 0)
    col = lax.broadcasted_iota(jnp.int32, (order, order), 1)
    diagonal = jnp.where(row == col, COEF_A, 0.0)
    factor = None
    for iteration in range(ITERS):
        moment_parts = split(moment)
        poly = diagonal + COEF_B * moment + COEF_C * product(moment_parts, moment_parts)
        poly_parts = split(poly)
        if factor is None:
            factor = poly * norm_inv
        else:
            factor = product(poly_parts, split(factor))
        if iteration + 1 < ITERS:
            moment = product(split(product(poly_parts, moment_parts)), poly_parts)
    update = dot(direction, factor.astype(jnp.bfloat16).T)
    update_ref[0] = (step_scale * update).astype(jnp.bfloat16)


def call(kernel, shapes, scratch=()):
    return pl.pallas_call(
        kernel,
        out_shape=shapes,
        scratch_shapes=scratch,
        compiler_params=pltpu.CompilerParams(vmem_limit_bytes=24 * 2**20),
    )


def per_device(grad, momentum):
    fsdp_count = lax.axis_size("fsdp")
    group_count = lax.axis_size("expert")
    _, width, order = grad.shape
    step_scale = 0.2 * math.sqrt(max(order, width * fsdp_count))
    count = grad.size * fsdp_count * group_count
    chips = fsdp_count // CORES
    share = len(blocks_of(order)) * LANE // fsdp_count
    f32 = jnp.float32
    parts, square = call(
        gram_kernel,
        (
            jax.ShapeDtypeStruct((fsdp_count, 3 * share, LANE), f32),
            jax.ShapeDtypeStruct((SUB, LANE), f32),
        ),
    )(grad, momentum)
    squares = lax.all_gather(square[0], "expert")
    parts = lax.all_to_all(parts, "fsdp", split_axis=0, concat_axis=0, tiled=True)
    pairs = [(i, i ^ 1) for i in range(fsdp_count)]
    groups = [[CORES * i + c for i in range(chips)] for c in range(CORES)]
    spread = call(
        middle_kernel, jax.ShapeDtypeStruct((chips, 3 * share + SUB, LANE), f32)
    )(parts, squares)
    mine = lax.all_to_all(
        spread, "fsdp", split_axis=0, concat_axis=0, tiled=True, axis_index_groups=groups
    )
    other = lax.ppermute(mine, "fsdp", pairs)
    return call(
        functools.partial(final_kernel, step_scale, count),
        (
            jax.ShapeDtypeStruct(grad.shape, f32),
            jax.ShapeDtypeStruct(grad.shape, jnp.bfloat16),
        ),
        (pltpu.VMEM((order, order), f32),),
    )(mine, other, grad, momentum)


def solution(mesh):
    placed = P("expert", "fsdp", None)
    return jax.shard_map(
        per_device,
        mesh=mesh,
        in_specs=(placed, placed),
        out_specs=(placed, placed),
        check_vma=False,
    )
```

```python
import functools
import math

import jax
import jax.numpy as jnp
from jax import lax
from jax.experimental import pallas as pl
from jax.experimental.pallas import tpu as pltpu
from jax.sharding import PartitionSpec as P

ITERS = 3

BETA = 0.95
COEF_A = 3.4445
COEF_B = -4.775
COEF_C = 2.0315

LANE = 128
SUB = 8
CORES = 2


def dot(a, b):
    return jnp.dot(a, b, preferred_element_type=jnp.float32)


def split(x):
    high = x.astype(jnp.bfloat16)
    return high, (x - high.astype(jnp.float32)).astype(jnp.bfloat16)


def blocks_of(order):
    side = order // LANE
    return [(i, j) for i in range(side) for j in range(i, side)]


def square_kernel(grad_ref, square_ref):
    full = grad_ref[0].astype(jnp.float32)
    squares = jnp.sum(full * full, axis=0, keepdims=True)
    square_ref[...] = jnp.broadcast_to(jnp.sum(squares, axis=1, keepdims=True), square_ref.shape)


def gram_kernel(grad_ref, momentum_ref, keep_ref, send_ref):
    core = lax.rem(lax.axis_index("fsdp"), CORES)
    grad = grad_ref[0]
    high, low = split(momentum_ref[0])
    grad_t, high_t, low_t = grad.T, high.T, low.T
    grams = (
        dot(grad_t, grad),
        (dot(grad_t, high) + dot(high_t, grad)) + (dot(grad_t, low) + dot(low_t, grad)),
        dot(high_t, high) + (dot(high_t, low) + dot(low_t, high)),
    )
    chips, rows, _ = keep_ref.shape
    per_gram = rows // len(grams)
    pieces = per_gram // SUB
    blocks = blocks_of(grad.shape[1])
    for which, gram in enumerate(grams):

        def piece(q):
            i, j = blocks[q // (LANE // SUB)]
            top = i * LANE + q % (LANE // SUB) * SUB
            return gram[top : top + SUB, j * LANE : (j + 1) * LANE]

        for chip in range(chips):
            for p in range(pieces):
                first = piece((chip * CORES) * pieces + p)
                second = piece((chip * CORES + 1) * pieces + p)
                at = pl.ds(which * per_gram + p * SUB, SUB)
                keep_ref[chip, at, :] = jnp.where(core == 0, first, second)
                send_ref[chip, at, :] = jnp.where(core == 0, second, first)


def middle_kernel(parts_ref, squares_ref, spread_ref):
    chips, rows, _ = parts_ref.shape
    total = jnp.sum(parts_ref[...], axis=0)
    squares = jnp.broadcast_to(squares_ref[...], (SUB, LANE))
    for chip in range(chips):
        spread_ref[chip, :rows, :] = total
        spread_ref[chip, rows:, :] = squares


def product(a, b):
    return dot(a[0], b[0]) + (dot(a[0], b[1]) + dot(a[1], b[0]))


def final_kernel(step_scale, count, mine_ref, other_ref, grad_ref, momentum_ref, new_ref, update_ref, gram_ref):
    core = lax.rem(lax.axis_index("fsdp"), CORES)
    order = grad_ref.shape[2]
    chips, rows, _ = mine_ref.shape
    per_gram = (rows - SUB) // 3
    pieces = per_gram // SUB
    squares = jnp.sum(mine_ref[:, rows - SUB :, :], axis=0) + jnp.sum(other_ref[:, rows - SUB :, :], axis=0)
    clip = 1.0 / jnp.sqrt(squares / count + 1e-06)
    alpha = (1.0 + BETA) * clip
    some = alpha > 0.0
    gain_gg, gain_gm, gain_mm = alpha * alpha, alpha * (BETA * BETA), BETA**4
    blocks = blocks_of(order)
    trace = jnp.zeros((SUB, LANE), jnp.float32)
    for chip in range(chips):
        for p in range(pieces):
            at = [pl.ds(which * per_gram + p * SUB, SUB) for which in range(3)]
            held = [mine_ref[chip, a, :] for a in at]
            came = [other_ref[chip, a, :] for a in at]

            def joined(gg, gm, mm):
                return jnp.where(some, gain_gg * gg + gain_gm * gm, 0.0) + gain_mm * mm

            held, came = joined(*held), joined(*came)
            for c, piece in ((0, jnp.where(core == 0, held, came)), (1, jnp.where(core == 0, came, held))):
                q = (chip * CORES + c) * pieces + p
                i, j = blocks[q // (LANE // SUB)]
                down = q % (LANE // SUB) * SUB
                gram_ref[i * LANE + down : i * LANE + down + SUB, j * LANE : (j + 1) * LANE] = piece
                if i == j:
                    row = lax.broadcasted_iota(jnp.int32, (SUB, LANE), 0) + down
                    col = lax.broadcasted_iota(jnp.int32, (SUB, LANE), 1)
                    trace = trace + jnp.where(row == col, piece, 0.0)
    for i, j in blocks:
        if i < j:
            gram_ref[j * LANE : (j + 1) * LANE, i * LANE : (i + 1) * LANE] = gram_ref[
                i * LANE : (i + 1) * LANE, j * LANE : (j + 1) * LANE
            ].T

    clip = clip[:1, :1]
    grad_full = grad_ref[0].astype(jnp.float32)
    new_momentum = BETA * momentum_ref[0] + clip * grad_full
    new_ref[0] = new_momentum
    direction = (clip * grad_full + BETA * new_momentum).astype(jnp.bfloat16)

    trace = jnp.sum(jnp.sum(trace, axis=0, keepdims=True), axis=1, keepdims=True)
    norm_inv = 1.0 / (jnp.sqrt(trace) + 1e-07)
    moment = gram_ref[...] * (norm_inv * norm_inv)
    row = lax.broadcasted_iota(jnp.int32, (order, order), 0)
    col = lax.broadcasted_iota(jnp.int32, (order, order), 1)
    diagonal = jnp.where(row == col, COEF_A, 0.0)
    factor = None
    for iteration in range(ITERS):
        moment_parts = split(moment)
        poly = diagonal + COEF_B * moment + COEF_C * product(moment_parts, moment_parts)
        poly_parts = split(poly)
        if factor is None:
            factor = poly * norm_inv
        else:
            factor = product(poly_parts, split(factor))
        if iteration + 1 < ITERS:
            moment = product(split(product(poly_parts, moment_parts)), poly_parts)
    update = dot(direction, factor.astype(jnp.bfloat16).T)
    update_ref[0] = (step_scale * update).astype(jnp.bfloat16)


def call(kernel, shapes, scratch=()):
    return pl.pallas_call(
        kernel,
        out_shape=shapes,
        scratch_shapes=scratch,
        compiler_params=pltpu.CompilerParams(vmem_limit_bytes=24 * 2**20),
    )


def per_device(grad, momentum):
    fsdp_count = lax.axis_size("fsdp")
    group_count = lax.axis_size("expert")
    _, width, order = grad.shape
    step_scale = 0.2 * math.sqrt(max(order, width * fsdp_count))
    count = grad.size * fsdp_count * group_count
    chips = fsdp_count // CORES
    share = len(blocks_of(order)) * LANE // fsdp_count
    f32 = jnp.float32
    half = jax.ShapeDtypeStruct((chips, 3 * share, LANE), f32)
    groups = [[CORES * i + c for i in range(chips)] for c in range(CORES)]

    def exchange(x):
        return lax.all_to_all(x, "fsdp", split_axis=0, concat_axis=0, tiled=True, axis_index_groups=groups)

    square = call(square_kernel, jax.ShapeDtypeStruct((chips, LANE), f32))(grad)
    plane = jnp.sum(exchange(square), axis=0, keepdims=True)
    turns = [
        (f * group_count + z, f * group_count + (z + f // CORES) % group_count)
        for f in range(fsdp_count)
        for z in range(group_count)
    ]
    planes = lax.ppermute(plane, ("fsdp", "expert"), turns)
    keep, send = call(gram_kernel, (half, half))(grad, momentum)
    pairs = [(i, i ^ 1) for i in range(fsdp_count)]
    both = keep + lax.ppermute(send, "fsdp", pairs)
    spread = call(
        middle_kernel, jax.ShapeDtypeStruct((chips, 3 * share + SUB, LANE), f32)
    )(exchange(both), planes)
    mine = exchange(spread)
    other = lax.ppermute(mine, "fsdp", pairs)
    return call(
        functools.partial(final_kernel, step_scale, count),
        (
            jax.ShapeDtypeStruct(grad.shape, f32),
            jax.ShapeDtypeStruct(grad.shape, jnp.bfloat16),
        ),
        (pltpu.VMEM((order, order), f32),),
    )(mine, other, grad, momentum)


def solution(mesh):
    placed = P("expert", "fsdp", None)
    return jax.shard_map(
        per_device,
        mesh=mesh,
        in_specs=(placed, placed),
        out_specs=(placed, placed),
        check_vma=False,
    )
```

```python
import functools
import math

import jax
import jax.numpy as jnp
from jax import lax
from jax.experimental import pallas as pl
from jax.experimental.pallas import tpu as pltpu
from jax.sharding import PartitionSpec as P

ITERS = 3

BETA = 0.95
COEF_A = 3.4445
COEF_B = -4.775
COEF_C = 2.0315

LANE = 128
SUB = 8
CORES = 2


def dot(a, b):
    return jnp.dot(a, b, preferred_element_type=jnp.float32)


def split(x):
    high = x.astype(jnp.bfloat16)
    return high, (x - high.astype(jnp.float32)).astype(jnp.bfloat16)


def blocks_of(order):
    side = order // LANE
    return [(i, j) for i in range(side) for j in range(i, side)]


def gram_kernel(grad_ref, momentum_ref, keep_ref, send_ref, square_ref, grad_in, momentum_in, sems):
    core = lax.rem(lax.axis_index("fsdp"), CORES)
    copies = [
        pltpu.make_async_copy(grad_ref.at[0], grad_in, sems.at[0]),
        pltpu.make_async_copy(momentum_ref.at[0], momentum_in, sems.at[1]),
    ]
    for copy in copies:
        copy.start()
    copies[0].wait()
    grad = grad_in[...]
    full = grad.astype(jnp.float32)
    squares = jnp.sum(full * full, axis=0, keepdims=True)
    square_ref[...] = jnp.broadcast_to(jnp.sum(squares, axis=1, keepdims=True), square_ref.shape)
    copies[1].wait()
    high, low = split(momentum_in[...])
    grad_t, high_t, low_t = grad.T, high.T, low.T
    grams = (
        dot(grad_t, grad),
        (dot(grad_t, high) + dot(high_t, grad)) + (dot(grad_t, low) + dot(low_t, grad)),
        dot(high_t, high) + (dot(high_t, low) + dot(low_t, high)),
    )
    chips, rows, _ = keep_ref.shape
    per_gram = rows // len(grams)
    pieces = per_gram // SUB
    blocks = blocks_of(grad.shape[1])
    for which, gram in enumerate(grams):

        def piece(q):
            i, j = blocks[q // (LANE // SUB)]
            top = i * LANE + q % (LANE // SUB) * SUB
            return gram[top : top + SUB, j * LANE : (j + 1) * LANE]

        for chip in range(chips):
            for p in range(pieces):
                first = piece((chip * CORES) * pieces + p)
                second = piece((chip * CORES + 1) * pieces + p)
                at = pl.ds(which * per_gram + p * SUB, SUB)
                keep_ref[chip, at, :] = jnp.where(core == 0, first, second)
                send_ref[chip, at, :] = jnp.where(core == 0, second, first)


def middle_kernel(parts_ref, squares_ref, spread_ref):
    chips, rows, _ = parts_ref.shape
    total = jnp.sum(parts_ref[...], axis=0)
    squares = jnp.broadcast_to(jnp.sum(squares_ref[...], axis=0, keepdims=True), (SUB, LANE))
    for chip in range(chips):
        spread_ref[chip, :rows, :] = total
        spread_ref[chip, rows:, :] = squares


def product(a, b):
    order = b[0].shape[1]
    cut = order - order % 256
    left = jnp.concatenate([a[0], a[1][:, cut:]], axis=1)
    rest = jnp.concatenate([b[0][cut:], jnp.zeros((order - cut, order), jnp.bfloat16)], axis=1)
    wide = dot(left, jnp.concatenate([jnp.concatenate(b, axis=1), rest], axis=0))
    return wide[:, :order] + (wide[:, order:] + dot(a[1][:, :cut], b[0][:cut]))


def final_kernel(step_scale, count, mine_ref, other_ref, grad_ref, momentum_ref, new_ref, update_ref, gram_ref, new_out, sem):
    core = lax.rem(lax.axis_index("fsdp"), CORES)
    order = grad_ref.shape[2]
    chips, rows, _ = mine_ref.shape
    per_gram = (rows - SUB) // 3
    pieces = per_gram // SUB
    squares = jnp.sum(mine_ref[:, rows - SUB :, :], axis=0) + jnp.sum(other_ref[:, rows - SUB :, :], axis=0)
    clip = 1.0 / jnp.sqrt(squares / count + 1e-06)
    alpha = (1.0 + BETA) * clip
    some = alpha > 0.0
    gain_gg, gain_gm, gain_mm = alpha * alpha, alpha * (BETA * BETA), BETA**4
    blocks = blocks_of(order)
    trace = jnp.zeros((SUB, LANE), jnp.float32)
    for chip in range(chips):
        for p in range(pieces):
            at = [pl.ds(which * per_gram + p * SUB, SUB) for which in range(3)]
            held = [mine_ref[chip, a, :] for a in at]
            came = [other_ref[chip, a, :] for a in at]

            def joined(gg, gm, mm):
                return jnp.where(some, gain_gg * gg + gain_gm * gm, 0.0) + gain_mm * mm

            held, came = joined(*held), joined(*came)
            for c, piece in ((0, jnp.where(core == 0, held, came)), (1, jnp.where(core == 0, came, held))):
                q = (chip * CORES + c) * pieces + p
                i, j = blocks[q // (LANE // SUB)]
                down = q % (LANE // SUB) * SUB
                gram_ref[i * LANE + down : i * LANE + down + SUB, j * LANE : (j + 1) * LANE] = piece
                if i == j:
                    row = lax.broadcasted_iota(jnp.int32, (SUB, LANE), 0) + down
                    col = lax.broadcasted_iota(jnp.int32, (SUB, LANE), 1)
                    trace = trace + jnp.where(row == col, piece, 0.0)
    for i, j in blocks:
        if i < j:
            gram_ref[j * LANE : (j + 1) * LANE, i * LANE : (i + 1) * LANE] = gram_ref[
                i * LANE : (i + 1) * LANE, j * LANE : (j + 1) * LANE
            ].T

    clip = clip[:1, :1]
    grad_full = grad_ref[0].astype(jnp.float32)
    new_momentum = BETA * momentum_ref[0] + clip * grad_full
    new_out[...] = new_momentum
    copy = pltpu.make_async_copy(new_out, new_ref.at[0], sem)
    copy.start()
    direction = (clip * grad_full + BETA * new_momentum).astype(jnp.bfloat16)

    trace = jnp.sum(jnp.sum(trace, axis=0, keepdims=True), axis=1, keepdims=True)
    norm_inv = 1.0 / (jnp.sqrt(trace) + 1e-07)
    moment = gram_ref[...] * (norm_inv * norm_inv)
    row = lax.broadcasted_iota(jnp.int32, (order, order), 0)
    col = lax.broadcasted_iota(jnp.int32, (order, order), 1)
    diagonal = jnp.where(row == col, COEF_A, 0.0)
    factor = None
    for iteration in range(ITERS):
        moment_parts = split(moment)
        poly = diagonal + COEF_B * moment + COEF_C * product(moment_parts, moment_parts)
        poly_parts = split(poly)
        if factor is None:
            factor = poly * norm_inv
        else:
            factor = product(poly_parts, split(factor))
        if iteration + 1 < ITERS:
            moment = product(split(product(poly_parts, moment_parts)), poly_parts)
    update = dot(direction, factor.astype(jnp.bfloat16).T)
    update_ref[0] = (step_scale * update).astype(jnp.bfloat16)
    copy.wait()


HBM = pl.BlockSpec(memory_space=pltpu.HBM)


def call(kernel, shapes, **specs):
    return pl.pallas_call(
        kernel,
        out_shape=shapes,
        compiler_params=pltpu.CompilerParams(vmem_limit_bytes=24 * 2**20),
        **specs,
    )


def per_device(grad, momentum):
    fsdp_count = lax.axis_size("fsdp")
    group_count = lax.axis_size("expert")
    _, width, order = grad.shape
    step_scale = 0.2 * math.sqrt(max(order, width * fsdp_count))
    count = grad.size * fsdp_count * group_count
    chips = fsdp_count // CORES
    share = len(blocks_of(order)) * LANE // fsdp_count
    f32 = jnp.float32
    half = jax.ShapeDtypeStruct((chips, 3 * share, LANE), f32)
    groups = [[CORES * i + c for i in range(chips)] for c in range(CORES)]

    def exchange(x):
        return lax.all_to_all(x, "fsdp", split_axis=0, concat_axis=0, tiled=True, axis_index_groups=groups)

    keep, send, square = pl.pallas_call(
        gram_kernel,
        out_shape=(half, half, jax.ShapeDtypeStruct((chips, LANE), f32)),
        compiler_params=pltpu.CompilerParams(vmem_limit_bytes=60 * 2**20),
        in_specs=[HBM, HBM],
        scratch_shapes=[
            pltpu.VMEM((width, order), grad.dtype),
            pltpu.VMEM((width, order), f32),
            pltpu.SemaphoreType.DMA((2,)),
        ],
    )(grad, momentum)
    plane = exchange(square)
    turns = [
        (f * group_count + z, f * group_count + (z + f // CORES) % group_count)
        for f in range(fsdp_count)
        for z in range(group_count)
    ]
    planes = lax.ppermute(plane, ("fsdp", "expert"), turns)
    pairs = [(i, i ^ 1) for i in range(fsdp_count)]
    both = keep + lax.ppermute(send, "fsdp", pairs)
    spread = call(
        middle_kernel, jax.ShapeDtypeStruct((chips, 3 * share + SUB, LANE), f32)
    )(exchange(both), planes)
    mine = exchange(spread)
    other = lax.ppermute(mine, "fsdp", pairs)
    return call(
        functools.partial(final_kernel, step_scale, count),
        (
            jax.ShapeDtypeStruct(grad.shape, f32),
            jax.ShapeDtypeStruct(grad.shape, jnp.bfloat16),
        ),
        out_specs=(HBM, pl.BlockSpec(memory_space=pltpu.VMEM)),
        scratch_shapes=[
            pltpu.VMEM((order, order), f32),
            pltpu.VMEM((width, order), f32),
            pltpu.SemaphoreType.DMA,
        ],
    )(mine, other, grad, momentum)


def solution(mesh):
    placed = P("expert", "fsdp", None)
    return jax.shard_map(
        per_device,
        mesh=mesh,
        in_specs=(placed, placed),
        out_specs=(placed, placed),
        check_vma=False,
    )
```

```python
import functools
import math

import jax
import jax.numpy as jnp
from jax import lax
from jax.experimental import pallas as pl
from jax.experimental.pallas import tpu as pltpu
from jax.sharding import PartitionSpec as P

ITERS = 3

BETA = 0.95
COEF_A = 3.4445
COEF_B = -4.775
COEF_C = 2.0315

LANE = 128
SUB = 8
CORES = 2
SPARE = 4


def dot(a, b):
    return jnp.dot(a, b, preferred_element_type=jnp.float32)


def split(x):
    high = x.astype(jnp.bfloat16)
    return high, (x - high.astype(jnp.float32)).astype(jnp.bfloat16)


def pairs_of(side):
    return [(i, j) for i in range(side) for j in range(i + 1, side)]


def places(shape):
    return lax.broadcasted_iota(jnp.int32, shape, 0), lax.broadcasted_iota(jnp.int32, shape, 1)


def block_of(gram, i, j):
    return gram[i * LANE : (i + 1) * LANE, j * LANE : (j + 1) * LANE]


def diagonal_of(block):
    row, col = places(block.shape)
    return jnp.sum(jnp.where(row == col, block, 0.0), axis=0, keepdims=True)


def gram_kernel(grad_ref, momentum_ref, keep_ref, send_ref, square_ref, grad_in, momentum_in, sems):
    core = lax.rem(lax.axis_index("fsdp"), CORES)
    copies = [
        pltpu.make_async_copy(grad_ref.at[0], grad_in, sems.at[0]),
        pltpu.make_async_copy(momentum_ref.at[0], momentum_in, sems.at[1]),
    ]
    for copy in copies:
        copy.start()
    copies[0].wait()
    grad = grad_in[...]
    full = grad.astype(jnp.float32)
    squares = jnp.sum(full * full, axis=0, keepdims=True)
    square_ref[...] = jnp.broadcast_to(jnp.sum(squares, axis=1, keepdims=True), square_ref.shape)
    copies[1].wait()
    high, low = split(momentum_in[...])
    grad_t, high_t, low_t = grad.T, high.T, low.T
    grams = (
        dot(grad_t, grad),
        (dot(grad_t, high) + dot(high_t, grad)) + (dot(grad_t, low) + dot(low_t, grad)),
        dot(high_t, high) + (dot(high_t, low) + dot(low_t, high)),
    )
    side = grad.shape[1] // LANE
    row, col = places((LANE, LANE))
    gg, gm, mm = [[block_of(gram, k, k) for k in range(side)] for gram in grams]
    packed = [jnp.where(row <= col, gg[k], gm[k]) for k in range(side)]
    packed += [jnp.where(row <= col, mm[0], mm[1]), mm[2]]
    packed += [block_of(gram, i, j) for gram in grams for i, j in pairs_of(side)]
    last = [diagonal_of(block) for block in gm + [mm[1]]]
    last = jnp.concatenate(last + [jnp.zeros((SUB - len(last), LANE), jnp.float32)], axis=0)
    chips, rows, _ = keep_ref.shape
    pieces = rows // SUB - 1

    def piece(q):
        top = q % (LANE // SUB) * SUB
        return packed[q // (LANE // SUB)][top : top + SUB]

    for chip in range(chips):
        for p in range(pieces):
            first = piece((chip * CORES) * pieces + p)
            second = piece((chip * CORES + 1) * pieces + p)
            keep_ref[chip, p * SUB : (p + 1) * SUB, :] = jnp.where(core == 0, first, second)
            send_ref[chip, p * SUB : (p + 1) * SUB, :] = jnp.where(core == 0, second, first)
        keep_ref[chip, pieces * SUB :, :] = last
        send_ref[chip, pieces * SUB :, :] = last


def middle_kernel(parts_ref, squares_ref, spread_ref):
    chips, rows, _ = parts_ref.shape
    total = jnp.sum(parts_ref[...], axis=0)
    squares = jnp.sum(squares_ref[...], axis=0, keepdims=True)
    row, _ = places((SUB, LANE))
    last = jnp.where(row == SPARE, squares, total[rows - SUB :])
    for chip in range(chips):
        spread_ref[chip, : rows - SUB, :] = total[: rows - SUB]
        spread_ref[chip, rows - SUB :, :] = last


def product(a, b):
    order = b[0].shape[1]
    cut = order - order % 256
    left = jnp.concatenate([a[0], a[1][:, cut:]], axis=1)
    rest = jnp.concatenate([b[0][cut:], jnp.zeros((order - cut, order), jnp.bfloat16)], axis=1)
    wide = dot(left, jnp.concatenate([jnp.concatenate(b, axis=1), rest], axis=0))
    return wide[:, :order] + (wide[:, order:] + dot(a[1][:, :cut], b[0][:cut]))


def final_kernel(step_scale, count, mine_ref, other_ref, grad_ref, momentum_ref, new_ref, update_ref, packed_ref, gram_ref, new_out, sem):
    core = lax.rem(lax.axis_index("fsdp"), CORES)
    order = grad_ref.shape[2]
    side = order // LANE
    chips, rows, _ = mine_ref.shape
    pieces = rows // SUB - 1
    squares = jnp.zeros((1, LANE), jnp.float32)
    for ref in (mine_ref, other_ref):
        squares = squares + jnp.sum(ref[:, rows - SUB :, :], axis=0)[SPARE : SPARE + 1]
    clip = 1.0 / jnp.sqrt(squares / count + 1e-06)
    alpha = (1.0 + BETA) * clip
    some = alpha > 0.0
    gain_gg, gain_gm, gain_mm = alpha * alpha, alpha * (BETA * BETA), BETA**4

    def grown(gain, block):
        return jnp.where(some, gain * block, 0.0)

    for chip in range(chips):
        for p in range(pieces):
            held = mine_ref[chip, p * SUB : (p + 1) * SUB, :]
            came = other_ref[chip, p * SUB : (p + 1) * SUB, :]
            for c, value in ((0, jnp.where(core == 0, held, came)), (1, jnp.where(core == 0, came, held))):
                q = (chip * CORES + c) * pieces + p
                packed_ref[q * SUB : (q + 1) * SUB, :] = value
    blocks = [packed_ref[k * LANE : (k + 1) * LANE, :] for k in range(packed_ref.shape[0] // LANE)]
    last = mine_ref[0, rows - SUB :, :]
    row, col = places((LANE, LANE))
    upper = jnp.where(row == col, 0.5, jnp.where(row < col, 1.0, 0.0))
    lower = jnp.where(row > col, 1.0, 0.0)
    half = jnp.where(row == col, 0.5, 0.0)
    trace = jnp.zeros((1, LANE), jnp.float32)
    for k in range(side):
        both = jnp.where(row > col, grown(gain_gm, blocks[k]), grown(gain_gg, blocks[k]) * jnp.where(row == col, 0.5, 1.0))
        both = both + half * grown(gain_gm, last[k : k + 1])
        if k == 0:
            both = both + gain_mm * (upper * blocks[side])
        elif k == 1:
            both = both + gain_mm * (lower * blocks[side] + half * last[side : side + 1])
        else:
            both = both + (0.5 * gain_mm) * blocks[side + 1]
        both = both + both.T
        trace = trace + diagonal_of(both)
        gram_ref[k * LANE : (k + 1) * LANE, k * LANE : (k + 1) * LANE] = both
    pairs = pairs_of(side)
    for n, (i, j) in enumerate(pairs):
        gg, gm, mm = [blocks[side + 2 + which * len(pairs) + n] for which in range(3)]
        block = grown(gain_gg, gg) + grown(gain_gm, gm) + gain_mm * mm
        gram_ref[i * LANE : (i + 1) * LANE, j * LANE : (j + 1) * LANE] = block
        gram_ref[j * LANE : (j + 1) * LANE, i * LANE : (i + 1) * LANE] = block.T

    clip = clip[:1, :1]
    grad_full = grad_ref[0].astype(jnp.float32)
    new_momentum = BETA * momentum_ref[0] + clip * grad_full
    new_out[...] = new_momentum
    copy = pltpu.make_async_copy(new_out, new_ref.at[0], sem)
    copy.start()
    direction = (clip * grad_full + BETA * new_momentum).astype(jnp.bfloat16)

    trace = jnp.sum(trace, axis=1, keepdims=True)
    norm_inv = 1.0 / (jnp.sqrt(trace) + 1e-07)
    moment = gram_ref[...] * (norm_inv * norm_inv)
    row = lax.broadcasted_iota(jnp.int32, (order, order), 0)
    col = lax.broadcasted_iota(jnp.int32, (order, order), 1)
    diagonal = jnp.where(row == col, COEF_A, 0.0)
    factor = None
    for iteration in range(ITERS):
        moment_parts = split(moment)
        poly = diagonal + COEF_B * moment + COEF_C * product(moment_parts, moment_parts)
        poly_parts = split(poly)
        if factor is None:
            factor = poly * norm_inv
        else:
            factor = product(poly_parts, split(factor))
        if iteration + 1 < ITERS:
            moment = product(split(product(poly_parts, moment_parts)), poly_parts)
    update = dot(direction, factor.astype(jnp.bfloat16).T)
    update_ref[0] = (step_scale * update).astype(jnp.bfloat16)
    copy.wait()


HBM = pl.BlockSpec(memory_space=pltpu.HBM)


def call(kernel, shapes, **specs):
    return pl.pallas_call(
        kernel,
        out_shape=shapes,
        compiler_params=pltpu.CompilerParams(vmem_limit_bytes=24 * 2**20),
        **specs,
    )


def per_device(grad, momentum):
    fsdp_count = lax.axis_size("fsdp")
    group_count = lax.axis_size("expert")
    _, width, order = grad.shape
    step_scale = 0.2 * math.sqrt(max(order, width * fsdp_count))
    count = grad.size * fsdp_count * group_count
    chips = fsdp_count // CORES
    side = order // LANE
    packed = (side + 2 + 3 * len(pairs_of(side))) * LANE
    share = packed // fsdp_count + SUB
    f32 = jnp.float32
    half = jax.ShapeDtypeStruct((chips, share, LANE), f32)
    groups = [[CORES * i + c for i in range(chips)] for c in range(CORES)]

    def exchange(x):
        return lax.all_to_all(x, "fsdp", split_axis=0, concat_axis=0, tiled=True, axis_index_groups=groups)

    keep, send, square = pl.pallas_call(
        gram_kernel,
        out_shape=(half, half, jax.ShapeDtypeStruct((chips, LANE), f32)),
        compiler_params=pltpu.CompilerParams(vmem_limit_bytes=60 * 2**20),
        in_specs=[HBM, HBM],
        scratch_shapes=[
            pltpu.VMEM((width, order), grad.dtype),
            pltpu.VMEM((width, order), f32),
            pltpu.SemaphoreType.DMA((2,)),
        ],
    )(grad, momentum)
    plane = exchange(square)
    turns = [
        (f * group_count + z, f * group_count + (z + f // CORES) % group_count)
        for f in range(fsdp_count)
        for z in range(group_count)
    ]
    planes = lax.ppermute(plane, ("fsdp", "expert"), turns)
    pairs = [(i, i ^ 1) for i in range(fsdp_count)]
    both = keep + lax.ppermute(send, "fsdp", pairs)
    spread = call(
        middle_kernel, half
    )(exchange(both), planes)
    mine = exchange(spread)
    other = lax.ppermute(mine, "fsdp", pairs)
    return call(
        functools.partial(final_kernel, step_scale, count),
        (
            jax.ShapeDtypeStruct(grad.shape, f32),
            jax.ShapeDtypeStruct(grad.shape, jnp.bfloat16),
        ),
        out_specs=(HBM, pl.BlockSpec(memory_space=pltpu.VMEM)),
        scratch_shapes=[
            pltpu.VMEM((packed, LANE), f32),
            pltpu.VMEM((order, order), f32),
            pltpu.VMEM((width, order), f32),
            pltpu.SemaphoreType.DMA,
        ],
    )(mine, other, grad, momentum)


def solution(mesh):
    placed = P("expert", "fsdp", None)
    return jax.shard_map(
        per_device,
        mesh=mesh,
        in_specs=(placed, placed),
        out_specs=(placed, placed),
        check_vma=False,
    )
```

```python
import functools
import math

import jax
import jax.numpy as jnp
from jax import lax
from jax.experimental import pallas as pl
from jax.experimental.pallas import tpu as pltpu
from jax.sharding import PartitionSpec as P

ITERS = 3

BETA = 0.95
COEF_A = 3.4445
COEF_B = -4.775
COEF_C = 2.0315

LANE = 128
SUB = 8
CORES = 2
SPARE = 4


def dot(a, b):
    return jnp.dot(a, b, preferred_element_type=jnp.float32)


def split(x):
    high = x.astype(jnp.bfloat16)
    return high, (x - high.astype(jnp.float32)).astype(jnp.bfloat16)


def pairs_of(side):
    return [(i, j) for i in range(side) for j in range(i + 1, side)]


def places(shape):
    return lax.broadcasted_iota(jnp.int32, shape, 0), lax.broadcasted_iota(jnp.int32, shape, 1)


def block_of(gram, i, j):
    return gram[i * LANE : (i + 1) * LANE, j * LANE : (j + 1) * LANE]


def diagonal_of(block):
    row, col = places(block.shape)
    return jnp.sum(jnp.where(row == col, block, 0.0), axis=0, keepdims=True)


def square_kernel(grad_ref, square_ref):
    full = grad_ref[0].astype(jnp.float32)
    squares = jnp.sum(full * full, axis=0, keepdims=True)
    square_ref[...] = jnp.broadcast_to(jnp.sum(squares, axis=1, keepdims=True), square_ref.shape)


def gram_kernel(grad_ref, momentum_ref, parts_ref, grad_in, momentum_in, sems):
    copies = [
        pltpu.make_async_copy(grad_ref.at[0], grad_in, sems.at[0]),
        pltpu.make_async_copy(momentum_ref.at[0], momentum_in, sems.at[1]),
    ]
    for copy in copies:
        copy.start()
    for copy in copies:
        copy.wait()
    grad = grad_in[...]
    high, low = split(momentum_in[...])
    grad_t, high_t, low_t = grad.T, high.T, low.T
    grams = (
        dot(grad_t, grad),
        (dot(grad_t, high) + dot(high_t, grad)) + (dot(grad_t, low) + dot(low_t, grad)),
        dot(high_t, high) + (dot(high_t, low) + dot(low_t, high)),
    )
    side = grad.shape[1] // LANE
    row, col = places((LANE, LANE))
    gg, gm, mm = [[block_of(gram, k, k) for k in range(side)] for gram in grams]
    packed = [jnp.where(row <= col, gg[k], gm[k]) for k in range(side)]
    packed += [jnp.where(row <= col, mm[0], mm[1]), mm[2]]
    packed += [block_of(gram, i, j) for gram in grams for i, j in pairs_of(side)]
    last = [diagonal_of(block) for block in gm + [mm[1]]]
    last = jnp.concatenate(last + [jnp.zeros((SUB - len(last), LANE), jnp.float32)], axis=0)
    devices, rows, _ = parts_ref.shape
    pieces = rows // SUB - 1
    for device in range(devices):
        for p in range(pieces):
            q = device * pieces + p
            top = q % (LANE // SUB) * SUB
            parts_ref[device, p * SUB : (p + 1) * SUB, :] = packed[q // (LANE // SUB)][top : top + SUB]
        parts_ref[device, pieces * SUB :, :] = last


def middle_kernel(parts_ref, squares_ref, spread_ref):
    chips, rows, _ = spread_ref.shape
    total = jnp.sum(parts_ref[...], axis=0)
    squares = jnp.sum(squares_ref[...], axis=0, keepdims=True)
    row, _ = places((SUB, LANE))
    last = jnp.where(row == SPARE, squares, total[rows - SUB :])
    for chip in range(chips):
        spread_ref[chip, : rows - SUB, :] = total[: rows - SUB]
        spread_ref[chip, rows - SUB :, :] = last


def product(a, b):
    order = b[0].shape[1]
    cut = order - order % 256
    left = jnp.concatenate([a[0], a[1][:, cut:]], axis=1)
    rest = jnp.concatenate([b[0][cut:], jnp.zeros((order - cut, order), jnp.bfloat16)], axis=1)
    wide = dot(left, jnp.concatenate([jnp.concatenate(b, axis=1), rest], axis=0))
    return wide[:, :order] + (wide[:, order:] + dot(a[1][:, :cut], b[0][:cut]))


def final_kernel(step_scale, count, mine_ref, other_ref, grad_ref, momentum_ref, new_ref, update_ref, packed_ref, gram_ref, new_out, sem):
    core = lax.rem(lax.axis_index("fsdp"), CORES)
    order = grad_ref.shape[2]
    side = order // LANE
    chips, rows, _ = mine_ref.shape
    pieces = rows // SUB - 1
    squares = jnp.zeros((1, LANE), jnp.float32)
    for ref in (mine_ref, other_ref):
        squares = squares + jnp.sum(ref[:, rows - SUB :, :], axis=0)[SPARE : SPARE + 1]
    clip = 1.0 / jnp.sqrt(squares / count + 1e-06)
    alpha = (1.0 + BETA) * clip
    some = alpha > 0.0
    gain_gg, gain_gm, gain_mm = alpha * alpha, alpha * (BETA * BETA), BETA**4

    def grown(gain, block):
        return jnp.where(some, gain * block, 0.0)

    for chip in range(chips):
        for p in range(pieces):
            held = mine_ref[chip, p * SUB : (p + 1) * SUB, :]
            came = other_ref[chip, p * SUB : (p + 1) * SUB, :]
            for c, value in ((0, jnp.where(core == 0, held, came)), (1, jnp.where(core == 0, came, held))):
                q = (chip * CORES + c) * pieces + p
                packed_ref[q * SUB : (q + 1) * SUB, :] = value
    blocks = [packed_ref[k * LANE : (k + 1) * LANE, :] for k in range(packed_ref.shape[0] // LANE)]
    last = mine_ref[0, rows - SUB :, :]
    row, col = places((LANE, LANE))
    upper = jnp.where(row == col, 0.5, jnp.where(row < col, 1.0, 0.0))
    lower = jnp.where(row > col, 1.0, 0.0)
    half = jnp.where(row == col, 0.5, 0.0)
    trace = jnp.zeros((1, LANE), jnp.float32)
    for k in range(side):
        both = jnp.where(row > col, grown(gain_gm, blocks[k]), grown(gain_gg, blocks[k]) * jnp.where(row == col, 0.5, 1.0))
        both = both + half * grown(gain_gm, last[k : k + 1])
        if k == 0:
            both = both + gain_mm * (upper * blocks[side])
        elif k == 1:
            both = both + gain_mm * (lower * blocks[side] + half * last[side : side + 1])
        else:
            both = both + (0.5 * gain_mm) * blocks[side + 1]
        both = both + both.T
        trace = trace + diagonal_of(both)
        gram_ref[k * LANE : (k + 1) * LANE, k * LANE : (k + 1) * LANE] = both
    pairs = pairs_of(side)
    for n, (i, j) in enumerate(pairs):
        gg, gm, mm = [blocks[side + 2 + which * len(pairs) + n] for which in range(3)]
        block = grown(gain_gg, gg) + grown(gain_gm, gm) + gain_mm * mm
        gram_ref[i * LANE : (i + 1) * LANE, j * LANE : (j + 1) * LANE] = block
        gram_ref[j * LANE : (j + 1) * LANE, i * LANE : (i + 1) * LANE] = block.T

    clip = clip[:1, :1]
    grad_full = grad_ref[0].astype(jnp.float32)
    new_momentum = BETA * momentum_ref[0] + clip * grad_full
    new_out[...] = new_momentum
    copy = pltpu.make_async_copy(new_out, new_ref.at[0], sem)
    copy.start()
    direction = (clip * grad_full + BETA * new_momentum).astype(jnp.bfloat16)

    trace = jnp.sum(trace, axis=1, keepdims=True)
    norm_inv = 1.0 / (jnp.sqrt(trace) + 1e-07)
    moment = gram_ref[...] * (norm_inv * norm_inv)
    row = lax.broadcasted_iota(jnp.int32, (order, order), 0)
    col = lax.broadcasted_iota(jnp.int32, (order, order), 1)
    diagonal = jnp.where(row == col, COEF_A, 0.0)
    factor = None
    for iteration in range(ITERS):
        moment_parts = split(moment)
        poly = diagonal + COEF_B * moment + COEF_C * product(moment_parts, moment_parts)
        poly_parts = split(poly)
        if factor is None:
            factor = poly * norm_inv
        else:
            factor = product(poly_parts, split(factor))
        if iteration + 1 < ITERS:
            moment = product(split(product(poly_parts, moment_parts)), poly_parts)
    update = dot(direction, factor.astype(jnp.bfloat16).T)
    update_ref[0] = (step_scale * update).astype(jnp.bfloat16)
    copy.wait()


HBM = pl.BlockSpec(memory_space=pltpu.HBM)


def call(kernel, shapes, **specs):
    return pl.pallas_call(
        kernel,
        out_shape=shapes,
        compiler_params=pltpu.CompilerParams(vmem_limit_bytes=24 * 2**20),
        **specs,
    )


def per_device(grad, momentum):
    fsdp_count = lax.axis_size("fsdp")
    group_count = lax.axis_size("expert")
    _, width, order = grad.shape
    step_scale = 0.2 * math.sqrt(max(order, width * fsdp_count))
    count = grad.size * fsdp_count * group_count
    chips = fsdp_count // CORES
    side = order // LANE
    packed = (side + 2 + 3 * len(pairs_of(side))) * LANE
    share = packed // fsdp_count + SUB
    f32 = jnp.float32
    half = jax.ShapeDtypeStruct((chips, share, LANE), f32)
    pairs = [(i, i ^ 1) for i in range(fsdp_count)]
    groups = [[CORES * i + c for i in range(chips)] for c in range(CORES)]

    def exchange(x, members=None):
        return lax.all_to_all(x, "fsdp", split_axis=0, concat_axis=0, tiled=True, axis_index_groups=members)

    turns = [
        (f * group_count + z, f * group_count + (z + f // CORES) % group_count)
        for f in range(fsdp_count)
        for z in range(group_count)
    ]
    square = call(square_kernel, jax.ShapeDtypeStruct((chips, LANE), f32))(grad)
    planes = lax.ppermute(exchange(square, members=groups), ("fsdp", "expert"), turns)
    parts = pl.pallas_call(
        gram_kernel,
        out_shape=jax.ShapeDtypeStruct((fsdp_count, share, LANE), f32),
        compiler_params=pltpu.CompilerParams(vmem_limit_bytes=60 * 2**20),
        in_specs=[HBM, HBM],
        scratch_shapes=[
            pltpu.VMEM((width, order), grad.dtype),
            pltpu.VMEM((width, order), f32),
            pltpu.SemaphoreType.DMA((2,)),
        ],
    )(grad, momentum)
    parts = exchange(parts)
    spread = call(
        middle_kernel, half
    )(parts, planes)
    mine = exchange(spread, members=groups)
    other = lax.ppermute(mine, "fsdp", pairs)
    return call(
        functools.partial(final_kernel, step_scale, count),
        (
            jax.ShapeDtypeStruct(grad.shape, f32),
            jax.ShapeDtypeStruct(grad.shape, jnp.bfloat16),
        ),
        out_specs=(HBM, pl.BlockSpec(memory_space=pltpu.VMEM)),
        scratch_shapes=[
            pltpu.VMEM((packed, LANE), f32),
            pltpu.VMEM((order, order), f32),
            pltpu.VMEM((width, order), f32),
            pltpu.SemaphoreType.DMA,
        ],
    )(mine, other, grad, momentum)


def solution(mesh):
    placed = P("expert", "fsdp", None)
    return jax.shard_map(
        per_device,
        mesh=mesh,
        in_specs=(placed, placed),
        out_specs=(placed, placed),
        check_vma=False,
    )
```

```python
import functools
import math

import jax
import jax.numpy as jnp
from jax import lax
from jax.experimental import pallas as pl
from jax.experimental.pallas import tpu as pltpu
from jax.sharding import PartitionSpec as P

ITERS = 3

BETA = 0.95
COEF_A = 3.4445
COEF_B = -4.775
COEF_C = 2.0315

LANE = 128
SUB = 8
CORES = 2
HALF = 64
SECOND = 96


def dot(a, b):
    return jnp.dot(a, b, preferred_element_type=jnp.float32)


def split(x):
    high = x.astype(jnp.bfloat16)
    return high, (x - high.astype(jnp.float32)).astype(jnp.bfloat16)


def pairs_of(side):
    return [(i, j) for i in range(side) for j in range(i + 1, side)]


def block_order(side):
    pairs = len(pairs_of(side))
    sizes = (pairs, side + 2, pairs, pairs)
    return [(sum(sizes[:n]), size) for n, size in enumerate(sizes)]


def places(shape):
    return lax.broadcasted_iota(jnp.int32, shape, 0), lax.broadcasted_iota(jnp.int32, shape, 1)


def block_of(gram, i, j):
    return gram[i * LANE : (i + 1) * LANE, j * LANE : (j + 1) * LANE]


def diagonal_of(block):
    row, col = places(block.shape)
    return jnp.sum(jnp.where(row == col, block, 0.0), axis=0, keepdims=True)


def with_diagonals(block, tile):
    row, col = places(tile.shape)
    free = col < HALF
    return jnp.concatenate(
        [
            block[:HALF],
            jnp.where(free, tile, block[HALF : HALF + SUB]),
            block[HALF + SUB : SECOND],
            jnp.where(free, pltpu.roll(tile, HALF, 1), block[SECOND : SECOND + SUB]),
            block[SECOND + SUB :],
        ],
        axis=0,
    )


def diagonals_in(block):
    row, col = places((SUB, LANE))
    second = pltpu.roll(block[SECOND : SECOND + SUB], HALF, 1)
    return jnp.where(col < HALF, block[HALF : HALF + SUB], second)


def square_kernel(grad_ref, square_ref):
    full = grad_ref[0].astype(jnp.float32)
    squares = jnp.sum(full * full, axis=0, keepdims=True)
    square_ref[...] = jnp.broadcast_to(jnp.sum(squares, axis=1, keepdims=True), square_ref.shape)


def gram_kernel(grad_ref, momentum_ref, parts_ref, grad_in, momentum_in, parts_out, sems):
    copies = [
        pltpu.make_async_copy(grad_ref.at[0], grad_in, sems.at[0]),
        pltpu.make_async_copy(momentum_ref.at[0], momentum_in, sems.at[1]),
    ]
    for copy in copies:
        copy.start()
    copies[0].wait()
    width, order = grad_in.shape
    side = order // LANE
    pairs = pairs_of(side)
    row, col = places((LANE, LANE))
    devices, rows, _ = parts_ref.shape
    pieces = rows // SUB
    per_block = LANE // SUB
    blocks, sent = [], [0]

    def deal(more):
        known = len(blocks) * per_block
        blocks.extend(more)
        for q in range(known, len(blocks) * per_block):
            device, p = divmod(q, pieces)
            top = q % per_block * SUB
            parts_out[device, p * SUB : (p + 1) * SUB, :] = blocks[q // per_block][top : top + SUB]
        done = len(blocks) * per_block // pieces
        at = pl.ds(sent[0], done - sent[0])
        copy = pltpu.make_async_copy(parts_out.at[at], parts_ref.at[at], sems.at[len(copies)])
        copy.start()
        copies.append(copy)
        sent[0] = done

    def tall(x):
        pad = -width % 256
        return jnp.concatenate([x, jnp.zeros((pad, order), x.dtype)], axis=0)

    def summed(*terms):
        return dot(
            jnp.concatenate([a for a, _ in terms], axis=1), jnp.concatenate([b for _, b in terms], axis=0)
        )

    grad = tall(grad_in[...])
    grad_t = grad.T
    gg = summed((grad_t, grad))
    deal([block_of(gg, i, j) for i, j in pairs])
    copies[1].wait()
    high, low = [tall(x) for x in split(momentum_in[...])]
    high_t, low_t = high.T, low.T
    mm = summed((high_t, high), (high_t, low), (low_t, high))
    gm = summed((grad_t, high), (high_t, grad), (grad_t, low), (low_t, grad))
    gg, gm_on, mm_on = [[block_of(gram, k, k) for k in range(side)] for gram in (gg, gm, mm)]
    last = [diagonal_of(block) for block in gm_on + [mm_on[1]]]
    last = jnp.concatenate(last + [jnp.zeros((SUB - len(last), LANE), jnp.float32)], axis=0)
    shared = [jnp.where(row <= col, gg[k], gm_on[k]) for k in range(side)]
    shared += [jnp.where(row <= col, mm_on[0], mm_on[1]), with_diagonals(mm_on[2], last)]
    deal(shared + [block_of(gm, i, j) for i, j in pairs])
    deal([block_of(mm, i, j) for i, j in pairs])
    for copy in copies[2:]:
        copy.wait()


def middle_kernel(parts_ref, squares_ref, spread_ref):
    chips, rows, _ = spread_ref.shape
    total = jnp.sum(parts_ref[...], axis=0)
    squares = jnp.sum(squares_ref[...], axis=0, keepdims=True)
    for chip in range(chips):
        spread_ref[chip, : rows - SUB, :] = total
        spread_ref[chip, rows - SUB :, :] = jnp.broadcast_to(squares, (SUB, LANE))


def product(a, b):
    order = b[0].shape[1]
    cut = order - order % 256
    left = jnp.concatenate([a[0], a[1][:, cut:]], axis=1)
    rest = jnp.concatenate([b[0][cut:], jnp.zeros((order - cut, order), jnp.bfloat16)], axis=1)
    wide = dot(left, jnp.concatenate([jnp.concatenate(b, axis=1), rest], axis=0))
    return wide[:, :order] + (wide[:, order:] + dot(a[1][:, :cut], b[0][:cut]))


def final_kernel(step_scale, count, mine_ref, other_ref, grad_ref, momentum_ref, new_ref, update_ref, gram_ref, new_out, sem):
    core = lax.rem(lax.axis_index("fsdp"), CORES)
    order = grad_ref.shape[2]
    side = order // LANE
    chips, rows, _ = mine_ref.shape
    pieces = rows // SUB - 1
    squares = jnp.zeros((1, LANE), jnp.float32)
    for ref in (mine_ref, other_ref):
        squares = squares + jnp.sum(ref[:, rows - SUB :, :], axis=0)[:1]
    clip = 1.0 / jnp.sqrt(squares / count + 1e-06)
    alpha = (1.0 + BETA) * clip
    some = alpha > 0.0
    gain_gg, gain_gm, gain_mm = alpha * alpha, alpha * (BETA * BETA), BETA**4

    def grown(gain, block):
        return jnp.where(some, gain * block, 0.0)


    def piece(q):
        chip, rest = divmod(q, CORES * pieces)
        c, p = divmod(rest, pieces)
        at = slice(p * SUB, (p + 1) * SUB)
        first, second = (mine_ref, other_ref) if c == 0 else (other_ref, mine_ref)
        return jnp.where(core == 0, first[chip, at, :], second[chip, at, :])

    per_block = LANE // SUB
    blocks = [
        jnp.concatenate([piece(k * per_block + n) for n in range(per_block)], axis=0)
        for k in range(chips * CORES * pieces // per_block)
    ]
    pairs = pairs_of(side)
    gg_pairs, packed, gm_pairs, mm_pairs = [
        blocks[at : at + size] for at, size in block_order(side)
    ]
    last = diagonals_in(packed[side + 1])
    row, col = places((LANE, LANE))
    upper = jnp.where(row == col, 0.5, jnp.where(row < col, 1.0, 0.0))
    lower = jnp.where(row > col, 1.0, 0.0)
    half = jnp.where(row == col, 0.5, 0.0)
    trace = jnp.zeros((1, LANE), jnp.float32)
    for k in range(side):
        both = jnp.where(row > col, grown(gain_gm, packed[k]), grown(gain_gg, packed[k]) * jnp.where(row == col, 0.5, 1.0))
        both = both + half * grown(gain_gm, last[k : k + 1])
        if k == 0:
            both = both + gain_mm * (upper * packed[side])
        elif k == 1:
            both = both + gain_mm * (lower * packed[side] + half * last[side : side + 1])
        else:
            both = both + gain_mm * jnp.where(row > col, 0.0, upper * packed[side + 1])
        trace = trace + 2.0 * diagonal_of(both)
        both = both + both.T
        gram_ref[k * LANE : (k + 1) * LANE, k * LANE : (k + 1) * LANE] = both
    for (i, j), gg, gm, mm in zip(pairs, gg_pairs, gm_pairs, mm_pairs):
        block = grown(gain_gg, gg) + grown(gain_gm, gm) + gain_mm * mm
        gram_ref[i * LANE : (i + 1) * LANE, j * LANE : (j + 1) * LANE] = block
        gram_ref[j * LANE : (j + 1) * LANE, i * LANE : (i + 1) * LANE] = block.T

    clip = clip[:1, :1]
    grad_full = grad_ref[0].astype(jnp.float32)
    new_momentum = BETA * momentum_ref[0] + clip * grad_full
    new_out[...] = new_momentum
    copy = pltpu.make_async_copy(new_out, new_ref.at[0], sem)
    copy.start()
    direction = (clip * grad_full + BETA * new_momentum).astype(jnp.bfloat16)

    trace = jnp.sum(trace, axis=1, keepdims=True)
    norm_inv = 1.0 / (jnp.sqrt(trace) + 1e-07)
    moment = gram_ref[...] * (norm_inv * norm_inv)
    row = lax.broadcasted_iota(jnp.int32, (order, order), 0)
    col = lax.broadcasted_iota(jnp.int32, (order, order), 1)
    diagonal = jnp.where(row == col, COEF_A, 0.0)
    factor = None
    for iteration in range(ITERS):
        moment_parts = split(moment)
        poly = diagonal + COEF_B * moment + COEF_C * product(moment_parts, moment_parts)
        poly_parts = split(poly)
        if factor is None:
            factor = poly * norm_inv
        else:
            factor = product(poly_parts, split(factor))
        if iteration + 1 < ITERS:
            moment = product(split(product(poly_parts, moment_parts)), poly_parts)
    update = dot(direction, factor.astype(jnp.bfloat16))
    update_ref[0] = (step_scale * update).astype(jnp.bfloat16)
    copy.wait()


HBM = pl.BlockSpec(memory_space=pltpu.HBM)


def call(kernel, shapes, **specs):
    return pl.pallas_call(
        kernel,
        out_shape=shapes,
        compiler_params=pltpu.CompilerParams(vmem_limit_bytes=24 * 2**20),
        **specs,
    )


def per_device(grad, momentum):
    fsdp_count = lax.axis_size("fsdp")
    group_count = lax.axis_size("expert")
    _, width, order = grad.shape
    step_scale = 0.2 * math.sqrt(max(order, width * fsdp_count))
    count = grad.size * fsdp_count * group_count
    chips = fsdp_count // CORES
    side = order // LANE
    packed = (side + 2 + 3 * len(pairs_of(side))) * LANE
    share = packed // fsdp_count
    f32 = jnp.float32
    spread = jax.ShapeDtypeStruct((chips, share + SUB, LANE), f32)
    pairs = [(i, i ^ 1) for i in range(fsdp_count)]
    groups = [[CORES * i + c for i in range(chips)] for c in range(CORES)]

    def exchange(x, members=None):
        return lax.all_to_all(x, "fsdp", split_axis=0, concat_axis=0, tiled=True, axis_index_groups=members)

    turns = [
        (f * group_count + z, f * group_count + (z + f) % group_count)
        for f in range(fsdp_count)
        for z in range(group_count)
    ]
    halves = [list(range(at, at + group_count)) for at in range(0, fsdp_count, group_count)]
    square = call(square_kernel, jax.ShapeDtypeStruct((group_count, LANE), f32))(grad)
    planes = lax.ppermute(exchange(square, halves), ("fsdp", "expert"), turns)
    parts = jax.ShapeDtypeStruct((fsdp_count, share, LANE), f32)
    parts = pl.pallas_call(
        gram_kernel,
        out_shape=parts,
        in_specs=[HBM, HBM],
        out_specs=HBM,
        scratch_shapes=[
            pltpu.VMEM((width, order), grad.dtype),
            pltpu.VMEM((width, order), f32),
            pltpu.VMEM(parts.shape, f32),
            pltpu.SemaphoreType.DMA((5,)),
        ],
        compiler_params=pltpu.CompilerParams(vmem_limit_bytes=60 * 2**20),
    )(grad, momentum)
    parts = exchange(parts)
    spread = call(middle_kernel, spread)(parts, planes)
    mine = exchange(spread, members=groups)
    other = lax.ppermute(mine, "fsdp", pairs)
    return call(
        functools.partial(final_kernel, step_scale, count),
        (
            jax.ShapeDtypeStruct(grad.shape, f32),
            jax.ShapeDtypeStruct(grad.shape, jnp.bfloat16),
        ),
        out_specs=(HBM, pl.BlockSpec(memory_space=pltpu.VMEM)),
        scratch_shapes=[
            pltpu.VMEM((order, order), f32),
            pltpu.VMEM((width, order), f32),
            pltpu.SemaphoreType.DMA,
        ],
    )(mine, other, grad, momentum)


def solution(mesh):
    placed = P("expert", "fsdp", None)
    return jax.shard_map(
        per_device,
        mesh=mesh,
        in_specs=(placed, placed),
        out_specs=(placed, placed),
        check_vma=False,
    )
```

```python
import functools
import math

import jax
import jax.numpy as jnp
from jax import lax
from jax.experimental import pallas as pl
from jax.experimental.pallas import tpu as pltpu
from jax.sharding import PartitionSpec as P

ITERS = 3

BETA = 0.95
COEF_A = 3.4445
COEF_B = -4.775
COEF_C = 2.0315

LANE = 128
SUB = 8
CORES = 2
ROW = 4
HALF = 64
SECOND = 96


def dot(a, b):
    return jnp.dot(a, b, preferred_element_type=jnp.float32)


def split(x):
    high = x.astype(jnp.bfloat16)
    return high, (x - high.astype(jnp.float32)).astype(jnp.bfloat16)


def pairs_of(side):
    return [(i, j) for i in range(side) for j in range(i + 1, side)]


def block_order(side):
    pairs = len(pairs_of(side))
    sizes = (pairs, side + 2, pairs, pairs)
    return [(sum(sizes[:n]), size) for n, size in enumerate(sizes)]


def places(shape):
    return lax.broadcasted_iota(jnp.int32, shape, 0), lax.broadcasted_iota(jnp.int32, shape, 1)


def block_of(gram, i, j):
    return gram[i * LANE : (i + 1) * LANE, j * LANE : (j + 1) * LANE]


def diagonal_of(block):
    row, col = places(block.shape)
    return jnp.sum(jnp.where(row == col, block, 0.0), axis=0, keepdims=True)


def with_diagonals(block, tile):
    row, col = places(tile.shape)
    free = col < HALF
    return jnp.concatenate(
        [
            block[:HALF],
            jnp.where(free, tile, block[HALF : HALF + SUB]),
            block[HALF + SUB : SECOND],
            jnp.where(free, pltpu.roll(tile, HALF, 1), block[SECOND : SECOND + SUB]),
            block[SECOND + SUB :],
        ],
        axis=0,
    )


def diagonals_in(block):
    row, col = places((SUB, LANE))
    second = pltpu.roll(block[SECOND : SECOND + SUB], HALF, 1)
    return jnp.where(col < HALF, block[HALF : HALF + SUB], second)


def square_kernel(grad_ref, square_ref):
    full = grad_ref[0].astype(jnp.float32)
    squares = jnp.sum(full * full, axis=0, keepdims=True)
    square_ref[...] = jnp.broadcast_to(jnp.sum(squares, axis=1, keepdims=True), square_ref.shape)


def gram_kernel(grad_ref, momentum_ref, parts_ref, grad_in, momentum_in, parts_out, sems):
    copies = [
        pltpu.make_async_copy(grad_ref.at[0], grad_in, sems.at[0]),
        pltpu.make_async_copy(momentum_ref.at[0], momentum_in, sems.at[1]),
    ]
    for copy in copies:
        copy.start()
    copies[0].wait()
    width, order = grad_in.shape
    side = order // LANE
    pairs = pairs_of(side)
    row, col = places((LANE, LANE))
    devices, rows, _ = parts_ref.shape
    pieces = rows // SUB
    per_block = LANE // SUB
    blocks, sent = [], [0]

    def deal(more):
        known = len(blocks) * per_block
        blocks.extend(more)
        for q in range(known, len(blocks) * per_block):
            device, p = divmod(q, pieces)
            top = q % per_block * SUB
            parts_out[device, p * SUB : (p + 1) * SUB, :] = blocks[q // per_block][top : top + SUB]
        done = len(blocks) * per_block // pieces
        at = pl.ds(sent[0], done - sent[0])
        copy = pltpu.make_async_copy(parts_out.at[at], parts_ref.at[at], sems.at[len(copies)])
        copy.start()
        copies.append(copy)
        sent[0] = done

    def tall(x):
        pad = -width % 256
        return jnp.concatenate([x, jnp.zeros((pad, order), x.dtype)], axis=0)

    def summed(*terms):
        return dot(
            jnp.concatenate([a for a, _ in terms], axis=1), jnp.concatenate([b for _, b in terms], axis=0)
        )

    grad = tall(grad_in[...])
    grad_t = grad.T
    gg = summed((grad_t, grad))
    deal([block_of(gg, i, j) for i, j in pairs])
    copies[1].wait()
    high, low = [tall(x) for x in split(momentum_in[...])]
    high_t, low_t = high.T, low.T
    mm = summed((high_t, high), (high_t, low), (low_t, high))
    gm = summed((grad_t, high), (high_t, grad), (grad_t, low), (low_t, grad))
    gg, gm_on, mm_on = [[block_of(gram, k, k) for k in range(side)] for gram in (gg, gm, mm)]
    last = [diagonal_of(block) for block in gm_on + [mm_on[1]]]
    last = jnp.concatenate(last + [jnp.zeros((SUB - len(last), LANE), jnp.float32)], axis=0)
    shared = [jnp.where(row <= col, gg[k], gm_on[k]) for k in range(side)]
    shared += [jnp.where(row <= col, mm_on[0], mm_on[1]), with_diagonals(mm_on[2], last)]
    deal(shared + [block_of(gm, i, j) for i, j in pairs])
    deal([block_of(mm, i, j) for i, j in pairs])
    for copy in copies[2:]:
        copy.wait()


def middle_kernel(parts_ref, squares_ref, spread_ref):
    chips, rows, _ = spread_ref.shape
    total = jnp.sum(parts_ref[...], axis=0)
    squares = jnp.sum(squares_ref[...], axis=0, keepdims=True)
    for chip in range(chips):
        spread_ref[chip, : rows - SUB, :] = total
        spread_ref[chip, rows - SUB :, :] = jnp.broadcast_to(squares, (SUB, LANE))


def product(a, b):
    order = b[0].shape[1]
    cut = order - order % 256
    left = jnp.concatenate([a[0], a[1][:, cut:]], axis=1)
    rest = jnp.concatenate([b[0][cut:], jnp.zeros((order - cut, order), jnp.bfloat16)], axis=1)
    wide = dot(left, jnp.concatenate([jnp.concatenate(b, axis=1), rest], axis=0))
    return wide[:, :order] + (wide[:, order:] + dot(a[1][:, :cut], b[0][:cut]))


def final_kernel(step_scale, count, mine_ref, other_ref, grad_ref, momentum_ref, new_ref, update_ref, gram_ref, new_out, sem):
    core = lax.rem(lax.axis_index("fsdp"), CORES)
    order = grad_ref.shape[2]
    side = order // LANE
    chips, rows, _ = mine_ref.shape
    pieces = rows // SUB - 1
    squares = jnp.zeros((1, LANE), jnp.float32)
    for ref in (mine_ref, other_ref):
        squares = squares + jnp.sum(ref[:, rows - SUB :, :], axis=0)[:1]
    clip = 1.0 / jnp.sqrt(squares / count + 1e-06)
    alpha = (1.0 + BETA) * clip
    some = alpha > 0.0
    gain_gg, gain_gm, gain_mm = alpha * alpha, alpha * (BETA * BETA), BETA**4

    def grown(gain, block):
        return jnp.where(some, gain * block, 0.0)


    def piece(q):
        chip, rest = divmod(q, CORES * pieces)
        c, p = divmod(rest, pieces)
        at = slice(p * SUB, (p + 1) * SUB)
        first, second = (mine_ref, other_ref) if c == 0 else (other_ref, mine_ref)
        return jnp.where(core == 0, first[chip, at, :], second[chip, at, :])

    per_block = LANE // SUB
    blocks = [
        jnp.concatenate([piece(k * per_block + n) for n in range(per_block)], axis=0)
        for k in range(chips * CORES * pieces // per_block)
    ]
    pairs = pairs_of(side)
    gg_pairs, packed, gm_pairs, mm_pairs = [
        blocks[at : at + size] for at, size in block_order(side)
    ]
    last = diagonals_in(packed[side + 1])
    row, col = places((LANE, LANE))
    upper = jnp.where(row == col, 0.5, jnp.where(row < col, 1.0, 0.0))
    lower = jnp.where(row > col, 1.0, 0.0)
    half = jnp.where(row == col, 0.5, 0.0)
    trace = jnp.zeros((1, LANE), jnp.float32)
    for k in range(side):
        both = jnp.where(row > col, grown(gain_gm, packed[k]), grown(gain_gg, packed[k]) * jnp.where(row == col, 0.5, 1.0))
        both = both + half * grown(gain_gm, last[k : k + 1])
        if k == 0:
            both = both + gain_mm * (upper * packed[side])
        elif k == 1:
            both = both + gain_mm * (lower * packed[side] + half * last[side : side + 1])
        else:
            both = both + gain_mm * jnp.where(row > col, 0.0, upper * packed[side + 1])
        trace = trace + 2.0 * diagonal_of(both)
        both = both + both.T
        gram_ref[k * LANE : (k + 1) * LANE, k * LANE : (k + 1) * LANE] = both
    for (i, j), gg, gm, mm in zip(pairs, gg_pairs, gm_pairs, mm_pairs):
        block = grown(gain_gg, gg) + grown(gain_gm, gm) + gain_mm * mm
        gram_ref[i * LANE : (i + 1) * LANE, j * LANE : (j + 1) * LANE] = block
        gram_ref[j * LANE : (j + 1) * LANE, i * LANE : (i + 1) * LANE] = block.T

    clip = clip[:1, :1]
    grad_full = grad_ref[0].astype(jnp.float32)
    new_momentum = BETA * momentum_ref[0] + clip * grad_full
    new_out[...] = new_momentum
    copy = pltpu.make_async_copy(new_out, new_ref.at[0], sem)
    copy.start()
    direction = (clip * grad_full + BETA * new_momentum).astype(jnp.bfloat16)

    trace = jnp.sum(trace, axis=1, keepdims=True)
    norm_inv = 1.0 / (jnp.sqrt(trace) + 1e-07)
    moment = gram_ref[...] * (norm_inv * norm_inv)
    row = lax.broadcasted_iota(jnp.int32, (order, order), 0)
    col = lax.broadcasted_iota(jnp.int32, (order, order), 1)
    diagonal = jnp.where(row == col, COEF_A, 0.0)
    factor = None
    for iteration in range(ITERS):
        moment_parts = split(moment)
        poly = diagonal + COEF_B * moment + COEF_C * product(moment_parts, moment_parts)
        poly_parts = split(poly)
        if factor is None:
            factor = poly * norm_inv
        else:
            factor = product(poly_parts, split(factor))
        if iteration + 1 < ITERS:
            moment = product(split(product(poly_parts, moment_parts)), poly_parts)
    update = dot(direction, factor.astype(jnp.bfloat16))
    update_ref[0] = (step_scale * update).astype(jnp.bfloat16)
    copy.wait()


HBM = pl.BlockSpec(memory_space=pltpu.HBM)


def call(kernel, shapes, **specs):
    return pl.pallas_call(
        kernel,
        out_shape=shapes,
        compiler_params=pltpu.CompilerParams(vmem_limit_bytes=24 * 2**20),
        **specs,
    )


def per_device(grad, momentum):
    fsdp_count = lax.axis_size("fsdp")
    group_count = lax.axis_size("expert")
    _, width, order = grad.shape
    step_scale = 0.2 * math.sqrt(max(order, width * fsdp_count))
    count = grad.size * fsdp_count * group_count
    chips = fsdp_count // CORES
    side = order // LANE
    packed = (side + 2 + 3 * len(pairs_of(side))) * LANE
    share = packed // fsdp_count
    f32 = jnp.float32
    spread = jax.ShapeDtypeStruct((chips, share + SUB, LANE), f32)
    pairs = [(i, i ^ 1) for i in range(fsdp_count)]
    groups = [[CORES * i + c for i in range(chips)] for c in range(CORES)]

    def exchange(x, members=None):
        return lax.all_to_all(x, "fsdp", split_axis=0, concat_axis=0, tiled=True, axis_index_groups=members)

    def hops(f):
        y, x = divmod(f // CORES, ROW)
        return min(y, fsdp_count // (CORES * ROW) - y) + min(x, ROW - x)

    ways = sorted(range(group_count), key=lambda k: -min(k, group_count - k))
    shift = {}
    for at in range(0, fsdp_count, group_count):
        shift.update(zip(sorted(range(at, at + group_count), key=hops), ways))
    turns = [
        (f * group_count + z, f * group_count + (z + shift[f]) % group_count)
        for f in range(fsdp_count)
        for z in range(group_count)
    ]
    halves = [list(range(at, at + group_count)) for at in range(0, fsdp_count, group_count)]
    square = call(square_kernel, jax.ShapeDtypeStruct((group_count, LANE), f32))(grad)
    planes = lax.ppermute(exchange(square, halves), ("fsdp", "expert"), turns)
    parts = jax.ShapeDtypeStruct((fsdp_count, share, LANE), f32)
    parts = pl.pallas_call(
        gram_kernel,
        out_shape=parts,
        in_specs=[HBM, HBM],
        out_specs=HBM,
        scratch_shapes=[
            pltpu.VMEM((width, order), grad.dtype),
            pltpu.VMEM((width, order), f32),
            pltpu.VMEM(parts.shape, f32),
            pltpu.SemaphoreType.DMA((5,)),
        ],
        compiler_params=pltpu.CompilerParams(vmem_limit_bytes=60 * 2**20),
    )(grad, momentum)
    parts = exchange(parts)
    spread = call(middle_kernel, spread)(parts, planes)
    mine = exchange(spread, members=groups)
    other = lax.ppermute(mine, "fsdp", pairs)
    return call(
        functools.partial(final_kernel, step_scale, count),
        (
            jax.ShapeDtypeStruct(grad.shape, f32),
            jax.ShapeDtypeStruct(grad.shape, jnp.bfloat16),
        ),
        out_specs=(HBM, pl.BlockSpec(memory_space=pltpu.VMEM)),
        scratch_shapes=[
            pltpu.VMEM((order, order), f32),
            pltpu.VMEM((width, order), f32),
            pltpu.SemaphoreType.DMA,
        ],
    )(mine, other, grad, momentum)


def solution(mesh):
    placed = P("expert", "fsdp", None)
    return jax.shard_map(
        per_device,
        mesh=mesh,
        in_specs=(placed, placed),
        out_specs=(placed, placed),
        check_vma=False,
    )
```

```python
import functools
import math

import jax
import jax.numpy as jnp
from jax import lax
from jax.experimental import pallas as pl
from jax.experimental.pallas import tpu as pltpu
from jax.sharding import PartitionSpec as P

ITERS = 3

BETA = 0.95
COEF_A = 3.4445
COEF_B = -4.775
COEF_C = 2.0315

LANE = 128
SUB = 8
CORES = 2
ROW = 4
HALF = 64
SECOND = 96


def dot(a, b):
    return jnp.dot(a, b, preferred_element_type=jnp.float32)


def split(x):
    high = x.astype(jnp.bfloat16)
    return high, (x - high.astype(jnp.float32)).astype(jnp.bfloat16)


def pairs_of(side):
    return [(i, j) for i in range(side) for j in range(i + 1, side)]


def block_order(side):
    pairs = len(pairs_of(side))
    sizes = (pairs, side + 2, pairs, pairs)
    return [(sum(sizes[:n]), size) for n, size in enumerate(sizes)]


def places(shape):
    return lax.broadcasted_iota(jnp.int32, shape, 0), lax.broadcasted_iota(jnp.int32, shape, 1)


def block_of(gram, i, j):
    return gram[i * LANE : (i + 1) * LANE, j * LANE : (j + 1) * LANE]


def diagonal_of(block):
    row, col = places(block.shape)
    return jnp.sum(jnp.where(row == col, block, 0.0), axis=0, keepdims=True)


def with_diagonals(block, tile):
    row, col = places(tile.shape)
    free = col < HALF
    return jnp.concatenate(
        [
            block[:HALF],
            jnp.where(free, tile, block[HALF : HALF + SUB]),
            block[HALF + SUB : SECOND],
            jnp.where(free, pltpu.roll(tile, HALF, 1), block[SECOND : SECOND + SUB]),
            block[SECOND + SUB :],
        ],
        axis=0,
    )


def diagonals_in(block):
    row, col = places((SUB, LANE))
    second = pltpu.roll(block[SECOND : SECOND + SUB], HALF, 1)
    return jnp.where(col < HALF, block[HALF : HALF + SUB], second)


def square_kernel(grad_ref, square_ref):
    full = grad_ref[0].astype(jnp.float32)
    squares = jnp.sum(full * full, axis=0, keepdims=True)
    square_ref[...] = jnp.broadcast_to(jnp.sum(squares, axis=1, keepdims=True), square_ref.shape)


def gram_kernel(grad_ref, momentum_ref, parts_ref, grad_in, momentum_in, parts_out, sems):
    copies = [
        pltpu.make_async_copy(grad_ref.at[0], grad_in, sems.at[0]),
        pltpu.make_async_copy(momentum_ref.at[0], momentum_in, sems.at[1]),
    ]
    for copy in copies:
        copy.start()
    copies[0].wait()
    width, order = grad_in.shape
    side = order // LANE
    pairs = pairs_of(side)
    row, col = places((LANE, LANE))
    devices, rows, _ = parts_ref.shape
    pieces = rows // SUB
    per_block = LANE // SUB
    blocks, sent = [], [0]

    def deal(more):
        known = len(blocks) * per_block
        blocks.extend(more)
        for q in range(known, len(blocks) * per_block):
            device, p = divmod(q, pieces)
            top = q % per_block * SUB
            parts_out[device, p * SUB : (p + 1) * SUB, :] = blocks[q // per_block][top : top + SUB]
        done = len(blocks) * per_block // pieces
        at = pl.ds(sent[0], done - sent[0])
        copy = pltpu.make_async_copy(parts_out.at[at], parts_ref.at[at], sems.at[len(copies)])
        copy.start()
        copies.append(copy)
        sent[0] = done

    def tall(x):
        pad = -width % 256
        return jnp.concatenate([x, jnp.zeros((pad, order), x.dtype)], axis=0)

    def summed(*terms):
        return dot(
            jnp.concatenate([a for a, _ in terms], axis=1), jnp.concatenate([b for _, b in terms], axis=0)
        )

    grad = tall(grad_in[...])
    grad_t = grad.T
    gg = summed((grad_t, grad))
    deal([block_of(gg, i, j) for i, j in pairs])
    copies[1].wait()
    high, low = [tall(x) for x in split(momentum_in[...])]
    high_t, low_t = high.T, low.T
    mm = summed((high_t, high), (high_t, low), (low_t, high))
    gm = summed((grad_t, high), (high_t, grad), (grad_t, low), (low_t, grad))
    gg, gm_on, mm_on = [[block_of(gram, k, k) for k in range(side)] for gram in (gg, gm, mm)]
    last = [diagonal_of(block) for block in gm_on + [mm_on[1]]]
    last = jnp.concatenate(last + [jnp.zeros((SUB - len(last), LANE), jnp.float32)], axis=0)
    shared = [jnp.where(row <= col, gg[k], gm_on[k]) for k in range(side)]
    shared += [jnp.where(row <= col, mm_on[0], mm_on[1]), with_diagonals(mm_on[2], last)]
    deal(shared + [block_of(gm, i, j) for i, j in pairs])
    deal([block_of(mm, i, j) for i, j in pairs])
    for copy in copies[2:]:
        copy.wait()


def middle_kernel(parts_ref, squares_ref, spread_ref):
    chips, rows, _ = spread_ref.shape
    total = jnp.sum(parts_ref[...], axis=0)
    squares = jnp.sum(squares_ref[...], axis=0, keepdims=True)
    for chip in range(chips):
        spread_ref[chip, : rows - SUB, :] = total
        spread_ref[chip, rows - SUB :, :] = jnp.broadcast_to(squares, (SUB, LANE))


def product(a, b):
    order = b[0].shape[1]
    cut = order - order % 256
    left = jnp.concatenate([a[0], a[1][:, cut:]], axis=1)
    rest = jnp.concatenate([b[0][cut:], jnp.zeros((order - cut, order), jnp.bfloat16)], axis=1)
    wide = dot(left, jnp.concatenate([jnp.concatenate(b, axis=1), rest], axis=0))
    return wide[:, :order] + (wide[:, order:] + dot(a[1][:, :cut], b[0][:cut]))


def final_kernel(step_scale, count, mine_ref, other_ref, grad_ref, momentum_ref, new_ref, update_ref, gram_ref, new_out, sem):
    core = lax.rem(lax.axis_index("fsdp"), CORES)
    order = grad_ref.shape[2]
    side = order // LANE
    chips, rows, _ = mine_ref.shape
    pieces = rows // SUB - 1
    squares = jnp.zeros((1, LANE), jnp.float32)
    for ref in (mine_ref, other_ref):
        squares = squares + jnp.sum(ref[:, rows - SUB :, :], axis=0)[:1]
    clip = 1.0 / jnp.sqrt(squares / count + 1e-06)
    alpha = (1.0 + BETA) * clip
    some = alpha > 0.0
    gain_gg, gain_gm, gain_mm = alpha * alpha, alpha * (BETA * BETA), BETA**4

    def grown(gain, block):
        return jnp.where(some, gain * block, 0.0)


    def piece(q):
        chip, rest = divmod(q, CORES * pieces)
        c, p = divmod(rest, pieces)
        at = slice(p * SUB, (p + 1) * SUB)
        first, second = (mine_ref, other_ref) if c == 0 else (other_ref, mine_ref)
        return jnp.where(core == 0, first[chip, at, :], second[chip, at, :])

    per_block = LANE // SUB
    blocks = [
        jnp.concatenate([piece(k * per_block + n) for n in range(per_block)], axis=0)
        for k in range(chips * CORES * pieces // per_block)
    ]
    pairs = pairs_of(side)
    gg_pairs, packed, gm_pairs, mm_pairs = [
        blocks[at : at + size] for at, size in block_order(side)
    ]
    last = diagonals_in(packed[side + 1])
    row, col = places((LANE, LANE))
    upper = jnp.where(row == col, 0.5, jnp.where(row < col, 1.0, 0.0))
    lower = jnp.where(row > col, 1.0, 0.0)
    half = jnp.where(row == col, 0.5, 0.0)
    trace = jnp.zeros((1, LANE), jnp.float32)
    for k in range(side):
        both = jnp.where(row > col, grown(gain_gm, packed[k]), grown(gain_gg, packed[k]) * jnp.where(row == col, 0.5, 1.0))
        both = both + half * grown(gain_gm, last[k : k + 1])
        if k == 0:
            both = both + gain_mm * (upper * packed[side])
        elif k == 1:
            both = both + gain_mm * (lower * packed[side] + half * last[side : side + 1])
        else:
            both = both + gain_mm * jnp.where(row > col, 0.0, upper * packed[side + 1])
        trace = trace + 2.0 * diagonal_of(both)
        both = both + both.T
        gram_ref[k * LANE : (k + 1) * LANE, k * LANE : (k + 1) * LANE] = both
    for (i, j), gg, gm, mm in zip(pairs, gg_pairs, gm_pairs, mm_pairs):
        block = grown(gain_gg, gg) + grown(gain_gm, gm) + gain_mm * mm
        gram_ref[i * LANE : (i + 1) * LANE, j * LANE : (j + 1) * LANE] = block
        gram_ref[j * LANE : (j + 1) * LANE, i * LANE : (i + 1) * LANE] = block.T

    clip = clip[:1, :1]
    grad_full = grad_ref[0].astype(jnp.float32)
    new_momentum = BETA * momentum_ref[0] + clip * grad_full
    new_out[...] = new_momentum
    copy = pltpu.make_async_copy(new_out, new_ref.at[0], sem)
    copy.start()
    direction = (clip * grad_full + BETA * new_momentum).astype(jnp.bfloat16)

    trace = jnp.sum(trace, axis=1, keepdims=True)
    norm_inv = 1.0 / (jnp.sqrt(trace) + 1e-07)
    moment = gram_ref[...] * (norm_inv * norm_inv)
    row = lax.broadcasted_iota(jnp.int32, (order, order), 0)
    col = lax.broadcasted_iota(jnp.int32, (order, order), 1)
    diagonal = jnp.where(row == col, COEF_A, 0.0)
    factor = None
    for iteration in range(ITERS):
        moment_parts = split(moment)
        poly = diagonal + COEF_B * moment + COEF_C * product(moment_parts, moment_parts)
        poly_parts = split(poly)
        if factor is None:
            factor = poly * norm_inv
        else:
            factor = product(poly_parts, split(factor))
        if iteration + 1 < ITERS:
            moment = product(split(product(poly_parts, moment_parts)), poly_parts)
    update = dot(direction, factor.astype(jnp.bfloat16))
    update_ref[0] = (step_scale * update).astype(jnp.bfloat16)
    copy.wait()


HBM = pl.BlockSpec(memory_space=pltpu.HBM)


def call(kernel, shapes, **specs):
    return pl.pallas_call(
        kernel,
        out_shape=shapes,
        compiler_params=pltpu.CompilerParams(vmem_limit_bytes=24 * 2**20),
        **specs,
    )


def per_device(grad, momentum):
    fsdp_count = lax.axis_size("fsdp")
    group_count = lax.axis_size("expert")
    _, width, order = grad.shape
    step_scale = 0.2 * math.sqrt(max(order, width * fsdp_count))
    count = grad.size * fsdp_count * group_count
    chips = fsdp_count // CORES
    side = order // LANE
    packed = (side + 2 + 3 * len(pairs_of(side))) * LANE
    share = packed // fsdp_count
    f32 = jnp.float32
    spread = jax.ShapeDtypeStruct((chips, share + SUB, LANE), f32)
    pairs = [(i, i ^ 1) for i in range(fsdp_count)]
    groups = [[CORES * i + c for i in range(chips)] for c in range(CORES)]

    def exchange(x, members=None):
        return lax.all_to_all(x, "fsdp", split_axis=0, concat_axis=0, tiled=True, axis_index_groups=members)

    def hops(f):
        y, x = divmod(f // CORES, ROW)
        return min(y, fsdp_count // (CORES * ROW) - y) + min(x, ROW - x)

    ways = sorted(range(group_count), key=lambda k: -min(k, group_count - k))
    shift = {}
    for at in range(0, fsdp_count, group_count):
        shift.update(zip(sorted(range(at, at + group_count), key=hops), ways))
    turns = [
        (f * group_count + z, f * group_count + (z + shift[f]) % group_count)
        for f in range(fsdp_count)
        for z in range(group_count)
    ]
    halves = [
        sorted(range(at, at + group_count), key=lambda f: abs(f // CORES % ROW - 1)) for at in range(0, fsdp_count, group_count)
    ]
    square = call(square_kernel, jax.ShapeDtypeStruct((group_count, LANE), f32))(grad)
    planes = lax.ppermute(exchange(square, halves), ("fsdp", "expert"), turns)
    parts = jax.ShapeDtypeStruct((fsdp_count, share, LANE), f32)
    parts = pl.pallas_call(
        gram_kernel,
        out_shape=parts,
        in_specs=[HBM, HBM],
        out_specs=HBM,
        scratch_shapes=[
            pltpu.VMEM((width, order), grad.dtype),
            pltpu.VMEM((width, order), f32),
            pltpu.VMEM(parts.shape, f32),
            pltpu.SemaphoreType.DMA((5,)),
        ],
        compiler_params=pltpu.CompilerParams(vmem_limit_bytes=60 * 2**20),
    )(grad, momentum)
    parts = exchange(parts)
    spread = call(middle_kernel, spread)(parts, planes)
    mine = exchange(spread, members=groups)
    other = lax.ppermute(mine, "fsdp", pairs)
    return call(
        functools.partial(final_kernel, step_scale, count),
        (
            jax.ShapeDtypeStruct(grad.shape, f32),
            jax.ShapeDtypeStruct(grad.shape, jnp.bfloat16),
        ),
        out_specs=(HBM, pl.BlockSpec(memory_space=pltpu.VMEM)),
        scratch_shapes=[
            pltpu.VMEM((order, order), f32),
            pltpu.VMEM((width, order), f32),
            pltpu.SemaphoreType.DMA,
        ],
    )(mine, other, grad, momentum)


def solution(mesh):
    placed = P("expert", "fsdp", None)
    return jax.shard_map(
        per_device,
        mesh=mesh,
        in_specs=(placed, placed),
        out_specs=(placed, placed),
        check_vma=False,
    )
```

```python
import functools
import math

import jax
import jax.numpy as jnp
from jax import lax
from jax.experimental import pallas as pl
from jax.experimental.pallas import tpu as pltpu
from jax.sharding import PartitionSpec as P

ITERS = 3

BETA = 0.95
COEF_A = 3.4445
COEF_B = -4.775
COEF_C = 2.0315

LANE = 128
SUB = 8
CORES = 2
ROW = 4
HALF = 64
SECOND = 96


def dot(a, b):
    return jnp.dot(a, b, preferred_element_type=jnp.float32)


def split(x):
    high = x.astype(jnp.bfloat16)
    return high, (x - high.astype(jnp.float32)).astype(jnp.bfloat16)


def pairs_of(side):
    return [(i, j) for i in range(side) for j in range(i + 1, side)]


def block_order(side):
    pairs = len(pairs_of(side))
    sizes = (pairs, side + 2, pairs, pairs)
    return [(sum(sizes[:n]), size) for n, size in enumerate(sizes)]


def places(shape):
    return lax.broadcasted_iota(jnp.int32, shape, 0), lax.broadcasted_iota(jnp.int32, shape, 1)


def block_of(gram, i, j):
    return gram[i * LANE : (i + 1) * LANE, j * LANE : (j + 1) * LANE]


def diagonal_of(block):
    row, col = places(block.shape)
    return jnp.sum(jnp.where(row == col, block, 0.0), axis=0, keepdims=True)


def with_diagonals(block, tile):
    row, col = places(tile.shape)
    free = col < HALF
    return jnp.concatenate(
        [
            block[:HALF],
            jnp.where(free, tile, block[HALF : HALF + SUB]),
            block[HALF + SUB : SECOND],
            jnp.where(free, pltpu.roll(tile, HALF, 1), block[SECOND : SECOND + SUB]),
            block[SECOND + SUB :],
        ],
        axis=0,
    )


def diagonals_in(block):
    row, col = places((SUB, LANE))
    second = pltpu.roll(block[SECOND : SECOND + SUB], HALF, 1)
    return jnp.where(col < HALF, block[HALF : HALF + SUB], second)


def square_kernel(grad_ref, square_ref):
    full = grad_ref[0].astype(jnp.float32)
    squares = jnp.sum(full * full, axis=0, keepdims=True)
    square_ref[...] = jnp.broadcast_to(jnp.sum(squares, axis=1, keepdims=True), square_ref.shape)


def gram_kernel(grad_ref, momentum_ref, parts_ref, grad_in, momentum_in, parts_out, sems):
    copies = [
        pltpu.make_async_copy(grad_ref.at[0], grad_in, sems.at[0]),
        pltpu.make_async_copy(momentum_ref.at[0], momentum_in, sems.at[1]),
    ]
    for copy in copies:
        copy.start()
    copies[0].wait()
    width, order = grad_in.shape
    side = order // LANE
    pairs = pairs_of(side)
    row, col = places((LANE, LANE))
    devices, rows, _ = parts_ref.shape
    pieces = rows // SUB
    per_block = LANE // SUB
    blocks, sent = [], [0]

    def deal(more):
        known = len(blocks) * per_block
        blocks.extend(more)
        for q in range(known, len(blocks) * per_block):
            device, p = divmod(q, pieces)
            top = q % per_block * SUB
            parts_out[device, p * SUB : (p + 1) * SUB, :] = blocks[q // per_block][top : top + SUB]
        done = len(blocks) * per_block // pieces
        at = pl.ds(sent[0], done - sent[0])
        copy = pltpu.make_async_copy(parts_out.at[at], parts_ref.at[at], sems.at[len(copies)])
        copy.start()
        copies.append(copy)
        sent[0] = done

    def tall(x):
        pad = -width % 256
        return jnp.concatenate([x, jnp.zeros((pad, order), x.dtype)], axis=0)

    def summed(*terms):
        return dot(
            jnp.concatenate([a for a, _ in terms], axis=1), jnp.concatenate([b for _, b in terms], axis=0)
        )

    grad = tall(grad_in[...])
    grad_t = grad.T
    gg = summed((grad_t, grad))
    deal([block_of(gg, i, j) for i, j in pairs])
    copies[1].wait()
    high, low = [tall(x) for x in split(momentum_in[...])]
    high_t, low_t = high.T, low.T
    mm = summed((high_t, high), (high_t, low), (low_t, high))
    gm = summed((grad_t, high), (high_t, grad), (grad_t, low), (low_t, grad))
    gg, gm_on, mm_on = [[block_of(gram, k, k) for k in range(side)] for gram in (gg, gm, mm)]
    last = [diagonal_of(block) for block in gm_on + [mm_on[1]]]
    last = jnp.concatenate(last + [jnp.zeros((SUB - len(last), LANE), jnp.float32)], axis=0)
    shared = [jnp.where(row <= col, gg[k], gm_on[k]) for k in range(side)]
    shared += [jnp.where(row <= col, mm_on[0], mm_on[1]), with_diagonals(mm_on[2], last)]
    deal(shared + [block_of(gm, i, j) for i, j in pairs])
    deal([block_of(mm, i, j) for i, j in pairs])
    for copy in copies[2:]:
        copy.wait()


def middle_kernel(parts_ref, squares_ref, spread_ref):
    chips, rows, _ = spread_ref.shape
    total = jnp.sum(parts_ref[...], axis=0)
    squares = jnp.sum(squares_ref[...], axis=0, keepdims=True)
    for chip in range(chips):
        spread_ref[chip, : rows - SUB, :] = total
        spread_ref[chip, rows - SUB :, :] = jnp.broadcast_to(squares, (SUB, LANE))


def product(a, b):
    order = b[0].shape[1]
    cut = order - order % 256
    left = jnp.concatenate([a[0], a[1][:, cut:]], axis=1)
    rest = jnp.concatenate([b[0][cut:], jnp.zeros((order - cut, order), jnp.bfloat16)], axis=1)
    wide = dot(left, jnp.concatenate([jnp.concatenate(b, axis=1), rest], axis=0))
    return wide[:, :order] + (wide[:, order:] + dot(a[1][:, :cut], b[0][:cut]))


def final_kernel(step_scale, count, mine_ref, other_ref, grad_ref, momentum_ref, new_ref, update_ref, gram_ref, new_out, sem):
    core = lax.rem(lax.axis_index("fsdp"), CORES)
    order = grad_ref.shape[2]
    side = order // LANE
    chips, rows, _ = mine_ref.shape
    pieces = rows // SUB - 1
    squares = jnp.zeros((1, LANE), jnp.float32)
    for ref in (mine_ref, other_ref):
        squares = squares + jnp.sum(ref[:, rows - SUB :, :], axis=0)[:1]
    clip = 1.0 / jnp.sqrt(squares / count + 1e-06)
    alpha = (1.0 + BETA) * clip
    some = alpha > 0.0
    gain_gg, gain_gm, gain_mm = alpha * alpha, alpha * (BETA * BETA), BETA**4

    def grown(gain, block):
        return jnp.where(some, gain * block, 0.0)


    def piece(q):
        chip, rest = divmod(q, CORES * pieces)
        c, p = divmod(rest, pieces)
        at = slice(p * SUB, (p + 1) * SUB)
        first, second = (mine_ref, other_ref) if c == 0 else (other_ref, mine_ref)
        return jnp.where(core == 0, first[seat[chip], at, :], second[seat[chip], at, :])

    seat = {chip: n for n, chip in enumerate(middle_first(chips))}
    per_block = LANE // SUB
    blocks = [
        jnp.concatenate([piece(k * per_block + n) for n in range(per_block)], axis=0)
        for k in range(chips * CORES * pieces // per_block)
    ]
    pairs = pairs_of(side)
    gg_pairs, packed, gm_pairs, mm_pairs = [
        blocks[at : at + size] for at, size in block_order(side)
    ]
    last = diagonals_in(packed[side + 1])
    row, col = places((LANE, LANE))
    upper = jnp.where(row == col, 0.5, jnp.where(row < col, 1.0, 0.0))
    lower = jnp.where(row > col, 1.0, 0.0)
    half = jnp.where(row == col, 0.5, 0.0)
    trace = jnp.zeros((1, LANE), jnp.float32)
    for k in range(side):
        both = jnp.where(row > col, grown(gain_gm, packed[k]), grown(gain_gg, packed[k]) * jnp.where(row == col, 0.5, 1.0))
        both = both + half * grown(gain_gm, last[k : k + 1])
        if k == 0:
            both = both + gain_mm * (upper * packed[side])
        elif k == 1:
            both = both + gain_mm * (lower * packed[side] + half * last[side : side + 1])
        else:
            both = both + gain_mm * jnp.where(row > col, 0.0, upper * packed[side + 1])
        trace = trace + 2.0 * diagonal_of(both)
        both = both + both.T
        gram_ref[k * LANE : (k + 1) * LANE, k * LANE : (k + 1) * LANE] = both
    for (i, j), gg, gm, mm in zip(pairs, gg_pairs, gm_pairs, mm_pairs):
        block = grown(gain_gg, gg) + grown(gain_gm, gm) + gain_mm * mm
        gram_ref[i * LANE : (i + 1) * LANE, j * LANE : (j + 1) * LANE] = block
        gram_ref[j * LANE : (j + 1) * LANE, i * LANE : (i + 1) * LANE] = block.T

    clip = clip[:1, :1]
    grad_full = grad_ref[0].astype(jnp.float32)
    new_momentum = BETA * momentum_ref[0] + clip * grad_full
    new_out[...] = new_momentum
    copy = pltpu.make_async_copy(new_out, new_ref.at[0], sem)
    copy.start()
    direction = (clip * grad_full + BETA * new_momentum).astype(jnp.bfloat16)

    trace = jnp.sum(trace, axis=1, keepdims=True)
    norm_inv = 1.0 / (jnp.sqrt(trace) + 1e-07)
    moment = gram_ref[...] * (norm_inv * norm_inv)
    row = lax.broadcasted_iota(jnp.int32, (order, order), 0)
    col = lax.broadcasted_iota(jnp.int32, (order, order), 1)
    diagonal = jnp.where(row == col, COEF_A, 0.0)
    factor = None
    for iteration in range(ITERS):
        moment_parts = split(moment)
        poly = diagonal + COEF_B * moment + COEF_C * product(moment_parts, moment_parts)
        poly_parts = split(poly)
        if factor is None:
            factor = poly * norm_inv
        else:
            factor = product(poly_parts, split(factor))
        if iteration + 1 < ITERS:
            moment = product(split(product(poly_parts, moment_parts)), poly_parts)
    update = dot(direction, factor.astype(jnp.bfloat16))
    update_ref[0] = (step_scale * update).astype(jnp.bfloat16)
    copy.wait()


HBM = pl.BlockSpec(memory_space=pltpu.HBM)


def middle_first(chips):
    return sorted(range(chips), key=lambda i: abs(i // ROW - 1) + abs(i % ROW - 1))


def call(kernel, shapes, **specs):
    return pl.pallas_call(
        kernel,
        out_shape=shapes,
        compiler_params=pltpu.CompilerParams(vmem_limit_bytes=24 * 2**20),
        **specs,
    )


def per_device(grad, momentum):
    fsdp_count = lax.axis_size("fsdp")
    group_count = lax.axis_size("expert")
    _, width, order = grad.shape
    step_scale = 0.2 * math.sqrt(max(order, width * fsdp_count))
    count = grad.size * fsdp_count * group_count
    chips = fsdp_count // CORES
    side = order // LANE
    packed = (side + 2 + 3 * len(pairs_of(side))) * LANE
    share = packed // fsdp_count
    f32 = jnp.float32
    spread = jax.ShapeDtypeStruct((chips, share + SUB, LANE), f32)
    pairs = [(i, i ^ 1) for i in range(fsdp_count)]
    groups = [[CORES * i + c for i in middle_first(chips)] for c in range(CORES)]

    def exchange(x, members=None):
        return lax.all_to_all(x, "fsdp", split_axis=0, concat_axis=0, tiled=True, axis_index_groups=members)

    def hops(f):
        y, x = divmod(f // CORES, ROW)
        return min(y, fsdp_count // (CORES * ROW) - y) + min(x, ROW - x)

    ways = sorted(range(group_count), key=lambda k: -min(k, group_count - k))
    shift = {}
    for at in range(0, fsdp_count, group_count):
        shift.update(zip(sorted(range(at, at + group_count), key=hops), ways))
    turns = [
        (f * group_count + z, f * group_count + (z + shift[f]) % group_count)
        for f in range(fsdp_count)
        for z in range(group_count)
    ]
    halves = [
        sorted(range(at, at + group_count), key=lambda f: abs(f // CORES % ROW - 1)) for at in range(0, fsdp_count, group_count)
    ]
    square = call(square_kernel, jax.ShapeDtypeStruct((group_count, LANE), f32))(grad)
    planes = lax.ppermute(exchange(square, halves), ("fsdp", "expert"), turns)
    parts = jax.ShapeDtypeStruct((fsdp_count, share, LANE), f32)
    parts = pl.pallas_call(
        gram_kernel,
        out_shape=parts,
        in_specs=[HBM, HBM],
        out_specs=HBM,
        scratch_shapes=[
            pltpu.VMEM((width, order), grad.dtype),
            pltpu.VMEM((width, order), f32),
            pltpu.VMEM(parts.shape, f32),
            pltpu.SemaphoreType.DMA((5,)),
        ],
        compiler_params=pltpu.CompilerParams(vmem_limit_bytes=60 * 2**20),
    )(grad, momentum)
    parts = exchange(parts)
    spread = call(middle_kernel, spread)(parts, planes)
    mine = exchange(spread, members=groups)
    other = lax.ppermute(mine, "fsdp", pairs)
    return call(
        functools.partial(final_kernel, step_scale, count),
        (
            jax.ShapeDtypeStruct(grad.shape, f32),
            jax.ShapeDtypeStruct(grad.shape, jnp.bfloat16),
        ),
        out_specs=(HBM, pl.BlockSpec(memory_space=pltpu.VMEM)),
        scratch_shapes=[
            pltpu.VMEM((order, order), f32),
            pltpu.VMEM((width, order), f32),
            pltpu.SemaphoreType.DMA,
        ],
    )(mine, other, grad, momentum)


def solution(mesh):
    placed = P("expert", "fsdp", None)
    return jax.shard_map(
        per_device,
        mesh=mesh,
        in_specs=(placed, placed),
        out_specs=(placed, placed),
        check_vma=False,
    )
```
